32 devices in a mesh: seq: 4 (over y, x), fsdp: 8 (over z, core).
Axes of the slice: x: 2, y: 2, z: 4, core: 2. Of those that a mesh axis runs over, the one named last changes fastest.
Arguments:
- hidden_in: bfloat16 [8, 1024, 1024], P('fsdp', 'seq'), may hold values from -3 to 3
- segment_ids: int32 [8, 1024], P('fsdp', 'seq'), may hold values from 0 to 3, never falling along the last dimension, each value on 1 to 512 neighbouring positions
- ln1_gain: bfloat16 [1024], P('fsdp'), may hold values from 0.099609375 to 1.8984375
- ln1_bias: bfloat16 [1024], P('fsdp'), may hold values from -3 to 3
- w_qkv: bfloat16 [1024, 3072], P('fsdp'), may hold values from -0.1875 to 0.1875
- b_qv: bfloat16 [2, 1024], P(None, 'fsdp'), may hold values from -3 to 3
- w_out: bfloat16 [1024, 1024], P('fsdp'), may hold values from -0.5 to 0.5
- b_out: bfloat16 [1024], P('fsdp'), may hold values from -3 to 3
- ln2_gain: bfloat16 [1024], P('fsdp'), may hold values from 0.099609375 to 1.8984375
- ln2_bias: bfloat16 [1024], P('fsdp'), may hold values from -3 to 3
- w_up: bfloat16 [1024, 4096], P('fsdp'), may hold values from -0.1875 to 0.1875
- b_up: bfloat16 [4096], P('fsdp'), may hold values from -3 to 3
- w_down: bfloat16 [4096, 1024], P('fsdp'), may hold values from -0.09375 to 0.09375
- b_down: bfloat16 [1024], P('fsdp'), may hold values from -3 to 3
- cotangent: bfloat16 [8, 1024, 1024], P('fsdp', 'seq'), may hold values from -6 to 6
Outputs:
- output: bfloat16 [8, 1024, 1024], P('fsdp', 'seq')
- grad_input: bfloat16 [8, 1024, 1024], P('fsdp', 'seq')
- grad_ln1_gain: float32 [1024], P('fsdp')
- grad_ln1_bias: float32 [1024], P('fsdp')
- grad_w_qkv: float32 [1024, 3072], P('fsdp')
- grad_b_qv: float32 [2, 1024], P(None, 'fsdp')
- grad_w_out: float32 [1024, 1024], P('fsdp')
- grad_b_out: float32 [1024], P('fsdp')
- grad_ln2_gain: float32 [1024], P('fsdp')
- grad_ln2_bias: float32 [1024], P('fsdp')
- grad_w_up: float32 [1024, 4096], P('fsdp')
- grad_b_up: float32 [4096], P('fsdp')
- grad_w_down: float32 [4096, 1024], P('fsdp')
- grad_b_down: float32 [1024], P('fsdp')
The draws below stay inside these ranges and needn't reach their ends.
Inputs may be any that keep to these rules, and one draw needn't show every extreme that they name: `segment_ids`: along each sequence the ids never fall; each of the 4 ids marks one run of consecutive tokens, the longest of them 1024 // 2 tokens.
All inputs are finite; a program needn't handle non-finite values.
Results may differ from the reference program's by a relative error of at most 0.02.
Values may be sent and summed in bfloat16 or wider, within the bound.
No kernel may reach another device: no remote copies, remote signals or barrier semaphores. Data moves between devices by JAX's collectives and lax.ppermute only.
A program may use at most 192 MiB of HBM per device.

```python
import math
import jax
import jax.numpy as jnp
import numpy as np
from jax import lax

D = 1024
H = 16
FF = 4096
DOCS = 4
LEN = 1024
SEQS = 8


def draw_hidden_in(key, part):
    jitter_key = jax.random.fold_in(key, 11)
    period_key = jax.random.fold_in(key, 12)
    phase_key = jax.random.fold_in(key, 13)
    places = jnp.arange(LEN, dtype=jnp.float32)
    periods = LEN * jnp.exp(jax.random.uniform(period_key, (D,), jnp.float32, math.log(0.5), math.log(2.0)))
    phases = jax.random.uniform(phase_key, (SEQS, 1, D), jnp.float32, -math.pi, math.pi)
    smooth_wave = jnp.cos(2.0 * math.pi * places[None, :, None] / periods[None, None, :] + phases)
    jitter = 0.6 * jax.random.truncated_normal(jitter_key, -3.0, 3.0, (SEQS, LEN, D), jnp.float32)
    return (jitter + 1.2 * smooth_wave).astype(jnp.bfloat16)


def level_of(key, dims, split, smallest, top_value):
    level = 1.0
    for position, parts in split:
        draws = jax.random.uniform(jax.random.fold_in(jax.random.fold_in(key, 6), position), (parts,), jnp.float32, smallest / len(split), top_value / len(split))
        level = level * jnp.repeat(jnp.exp(draws), dims[position] // parts).reshape((-1,) + (1,) * (len(dims) - 1 - position))
    return level


def split_up(amount, total, most, skew):
    weights = [(1 << 20) // math.isqrt(grade ** skew) + 1 for grade in range(2, amount + 1)]
    rest, holding = total - most - (amount - 1), [1] * (amount - 1)
    while rest > 0:
        movable = [i for i in range(amount - 1) if holding[i] < most]
        pool, left = sum([weights[i] for i in movable]), rest
        for i in movable:
            extra = min(most - holding[i], max(1, left * weights[i] // pool), rest)
            holding[i] = holding[i] + extra
            rest = rest - extra
    return np.array([most] + holding)


def ragged(own_key, count, total, reach, skew):
    if count == 2:
        one = jax.random.randint(own_key, (), max(1, total - reach), min(reach, total - 1) + 1)
        return jnp.stack([one, total - one])
    tallies = jnp.asarray(split_up(count, total, reach, skew), jnp.int32)
    pairs = (count - 1) // 2
    giver, receiver = tallies[1:1 + 2 * pairs:2], tallies[2:2 + 2 * pairs:2]
    slack = jnp.minimum(giver - 1, reach - receiver)
    moved = jax.random.randint(jax.random.fold_in(own_key, 1), (pairs,), 0, 1 << 20) % (slack + 1)
    tallies = tallies.at[1:1 + 2 * pairs:2].set(giver - moved).at[2:2 + 2 * pairs:2].set(receiver + moved)
    return tallies[jax.random.permutation(jax.random.fold_in(own_key, 2), count)]


def bell_draw(key, shape, deviation, reach, split=(), kind=jnp.bfloat16):
    array = deviation * jax.random.normal(key, shape, jnp.float32)
    if split:
        array = array * level_of(key, shape, split, -0.22, 0.18)
    return jnp.clip(array, -reach, reach).astype(kind)


def setup_inputs(seed: int = 0) -> dict:
    key_of = jax.random.split(jax.random.key(seed), 16)
    return {
        "hidden_in": draw_hidden_in(jax.random.fold_in(key_of[15], 71), 0),
        "segment_ids": jax.vmap(lambda own: jnp.searchsorted(jnp.cumsum(ragged(own, DOCS, LEN, LEN // 2, 2)), jnp.arange(LEN), side="right"))(jax.random.split(key_of[1], SEQS)).reshape((SEQS, LEN)).astype(jnp.int32),
        "ln1_gain": jnp.clip(1.0 + 0.18 * jax.random.normal(key_of[2], (D,), jnp.float32), 0.099609375, 1.8984375).astype(jnp.bfloat16),
        "ln1_bias": bell_draw(key_of[3], (D,), 0.5, 3.0, ((0, 8),)),
        "w_qkv": bell_draw(key_of[4], (D, 3 * D), D ** -0.5, 0.1875, ((0, 8),)),
        "b_qv": bell_draw(key_of[5], (2, D), 0.5, 3.0, ((1, 8),)),
        "w_out": bell_draw(key_of[6], (D, D), (D // 8) ** -0.5, 0.5, ((0, 8),)),
        "b_out": bell_draw(key_of[7], (D,), 0.5, 3.0, ((0, 8),)),
        "ln2_gain": jnp.clip(1.0 + 0.18 * jax.random.normal(key_of[8], (D,), jnp.float32), 0.099609375, 1.8984375).astype(jnp.bfloat16),
        "ln2_bias": bell_draw(key_of[9], (D,), 0.5, 3.0, ((0, 8),)),
        "w_up": bell_draw(key_of[10], (D, FF), D ** -0.5, 0.1875, ((0, 8),)),
        "b_up": bell_draw(key_of[11], (FF,), 0.5, 3.0, ((0, 8),)),
        "w_down": bell_draw(key_of[12], (FF, D), FF ** -0.5, 0.09375, ((0, 8),)),
        "b_down": bell_draw(key_of[13], (D,), 0.5, 3.0, ((0, 8),)),
        "cotangent": bell_draw(key_of[14], (SEQS, LEN, D), 1.0, 6.0, ((0, 8), (1, 4))),
    }


@jax.custom_vjp
def low(v):
    return lax.optimization_barrier(v.astype(jnp.bfloat16)).astype(jnp.float32)

@jax.custom_vjp
def low_back(v):
    return v

def low_keep(v):
    return (low(v), None)

def low_pass(kept, grad):
    return (grad,)

def back_keep(v):
    return (v, None)

def back_low(kept, grad):
    return (low(grad),)
low.defvjp(low_keep, low_pass)
low_back.defvjp(back_keep, back_low)
EPSILON = 1e-05

def exact(left_side, right_side):
    return jnp.dot(left_side, right_side, precision=lax.Precision.HIGHEST, preferred_element_type=jnp.float32)

def normalize(values, gain, shift):
    center = values - lax.optimization_barrier(jnp.mean(values, axis=-1, keepdims=True))
    spread = lax.optimization_barrier(jnp.mean(center * center, axis=-1, keepdims=True))
    return center * lax.rsqrt(spread + EPSILON) * gain + shift

def forward(tokens, weights_all, doc_ids):
    gain_one, shift_one, w_qkv, b_qv, w_out, b_out, gain_two, shift_two, w_up, b_up, w_down, b_down = weights_all
    length = tokens.shape[0]
    head_size = D // H
    score_scale = head_size ** (-0.5)
    normed = low(normalize(tokens, gain_one, shift_one))
    qkv_bias = jnp.concatenate([b_qv[0], jnp.zeros((D,), jnp.float32), b_qv[1]])
    projected = low(low_back(exact(normed, w_qkv) + qkv_bias))
    queries = projected[:, :D].reshape(length, H, head_size).transpose(1, 0, 2)
    keys_all = projected[:, D:2 * D].reshape(length, H, head_size).transpose(1, 0, 2)
    values_all = projected[:, 2 * D:].reshape(length, H, head_size).transpose(1, 0, 2)
    places = jnp.arange(length, dtype=jnp.int32)
    distance = (places[:, None] - places[None, :]).astype(jnp.float32)
    allowed = (places[None, :] <= places[:, None]) & (doc_ids[:, None] == doc_ids[None, :])
    slopes = 2.0 ** (-8.0 * (jnp.arange(H) + 1).astype(jnp.float32) / H)

    def one_head(inputs):
        query_head, key_head, value_head, slope = inputs
        raw = exact(query_head, key_head.T) * score_scale - slope * distance
        raw = low_back(raw)
        masked = jnp.where(allowed, raw, -1e+30)
        probs = jax.nn.softmax(masked, axis=-1)
        return exact(low(probs), value_head)
    context = lax.map(jax.checkpoint(one_head), (queries, keys_all, values_all, slopes))
    context = low(low_back(context.transpose(1, 0, 2).reshape(length, D)))
    attended = low_back(exact(context, w_out) + b_out)
    first_sum = tokens + attended
    normed_two = low(normalize(first_sum, gain_two, shift_two))
    upward = low_back(exact(normed_two, w_up) + b_up)
    activated = low(jax.nn.gelu(upward, approximate=True))
    branch = low_back(exact(activated, w_down) + b_down)
    return first_sum + branch

def reference(hidden_in, segment_ids, ln1_gain, ln1_bias, w_qkv, b_qv, w_out, b_out, ln2_gain, ln2_bias, w_up, b_up, w_down, b_down, cotangent):
    params = (ln1_gain.astype(jnp.float32), ln1_bias.astype(jnp.float32), w_qkv.astype(jnp.float32), b_qv.astype(jnp.float32), w_out.astype(jnp.float32), b_out.astype(jnp.float32), ln2_gain.astype(jnp.float32), ln2_bias.astype(jnp.float32), w_up.astype(jnp.float32), b_up.astype(jnp.float32), w_down.astype(jnp.float32), b_down.astype(jnp.float32))

    def per_sequence(totals, inputs):
        tokens, grad_top, doc_ids = inputs

        def layer(token_values, weight_values):
            return forward(token_values, weight_values, doc_ids)
        result, pullback = jax.vjp(layer, tokens.astype(jnp.float32), params)
        grad_tokens, grad_weights = pullback(grad_top.astype(jnp.float32))
        totals = jax.tree.map(jnp.add, totals, grad_weights)
        return (totals, (result.astype(jnp.bfloat16), grad_tokens.astype(jnp.bfloat16)))
    initial = jax.tree.map(jnp.zeros_like, params)
    totals, (outputs, grads_in) = lax.scan(per_sequence, initial, (hidden_in, cotangent, segment_ids))
    return (outputs, grads_in, totals[0], totals[1], totals[2], totals[3], totals[4], totals[5], totals[6], totals[7], totals[8], totals[9], totals[10], totals[11])
```

```python
import functools

import jax
import jax.numpy as jnp
from jax import lax
from jax.experimental import pallas as pl
from jax.experimental.pallas import tpu as pltpu
from jax.sharding import PartitionSpec as P

D = 1024
H = 16
HEAD = D // H
EPSILON = 1e-05
F32 = jnp.float32
BF16 = jnp.bfloat16
NT = (((1,), (1,)), ((), ()))
NN = (((1,), (0,)), ((), ()))
TN = (((0,), (0,)), ((), ()))


def dot(a, b, dims=NN):
    return lax.dot_general(a, b, dims, preferred_element_type=F32)


def key_start(first_query, block, longest):
    return max(0, (first_query - longest + 1) // block * block)


def masked_distance(seg_col, seg_row, k0, nk, q0, bq):
    key_at = lax.broadcasted_iota(jnp.int32, (nk, bq), 0) + k0
    query_at = lax.broadcasted_iota(jnp.int32, (nk, bq), 1) + q0
    ok = (key_at <= query_at) & (seg_col[k0 : k0 + nk, :] == seg_row[:, q0 : q0 + bq])
    return jnp.where(ok, (query_at - key_at).astype(F32), 1e32)


def only_head(values, head):
    lane = lax.broadcasted_iota(jnp.int32, values.shape, 1)
    return jnp.where(lane // HEAD == head, values, jnp.zeros_like(values))


def attention_kernel(slopes, proj, seg_col, seg_row, context, log_total, *, block, longest):
    length = proj.shape[0]
    width = proj.shape[1] // 3
    for q0 in range(0, length, block):
        k0 = key_start(q0, block, longest)
        nk = q0 + block - k0
        far = masked_distance(seg_col, seg_row, k0, nk, q0, block)
        queries = proj[q0 : q0 + block, :width] * BF16(HEAD**-0.5)
        keys = proj[k0 : k0 + nk, width : 2 * width]
        values = proj[k0 : k0 + nk, 2 * width :].T
        parts = []
        for head in range(width // HEAD):
            raw = dot(keys, only_head(queries, head), NT) - slopes[head] * far
            highest = jnp.max(raw, axis=0, keepdims=True)
            weights = jnp.exp(raw - highest)
            total = jnp.sum(weights, axis=0, keepdims=True)
            probs = (weights * (1.0 / total)).astype(BF16)
            log_total[head : head + 1, q0 : q0 + block] = highest + jnp.log(total)
            parts.append(dot(values[head * HEAD : (head + 1) * HEAD, :], probs))
        context[q0 : q0 + block, :] = jnp.concatenate(parts, axis=0).T.astype(BF16)


def attention_back_kernel(
    slopes, proj, grad, seg_col, seg_row, log_total, out, probs_all, scores_all, grad_keys, grad_values, *, block, longest
):
    length = proj.shape[0]
    width = proj.shape[1] // 3
    heads = width // HEAD
    grad_keys[...] = jnp.zeros_like(grad_keys)
    grad_values[...] = jnp.zeros_like(grad_values)
    for q0 in range(0, length, block):
        k0 = key_start(q0, block, longest)
        nk = q0 + block - k0
        far = masked_distance(seg_col, seg_row, k0, nk, q0, block)
        queries = proj[q0 : q0 + block, :width] * BF16(HEAD**-0.5)
        keys = proj[k0 : k0 + nk, width : 2 * width]
        values = proj[k0 : k0 + nk, 2 * width :]
        keys_t = keys.T
        tops = grad[q0 : q0 + block, :]
        parts, query_rows, top_rows = [], [], []
        for head in range(heads):
            query_head = only_head(queries, head)
            top_head = only_head(tops, head)
            query_rows.append(query_head)
            top_rows.append(top_head)
            raw = dot(keys, query_head, NT) - slopes[head] * far
            probs = jnp.exp(raw - log_total[head : head + 1, q0 : q0 + block])
            probs_all[:nk, head * block : (head + 1) * block] = probs.astype(BF16)
            grad_probs = dot(values, top_head, NT)
            row_sum = jnp.sum(probs * grad_probs, axis=0, keepdims=True)
            scores = (probs * (grad_probs - row_sum)).astype(BF16)
            scores_all[:nk, head * block : (head + 1) * block] = scores
            parts.append(dot(keys_t[head * HEAD : (head + 1) * HEAD, :], scores))
        grad_values[k0 : k0 + nk, :] += dot(probs_all[:nk, :], jnp.concatenate(top_rows, axis=0))
        grad_keys[k0 : k0 + nk, :] += dot(scores_all[:nk, :], jnp.concatenate(query_rows, axis=0))
        out[q0 : q0 + block, :width] = (jnp.concatenate(parts, axis=0).T * HEAD**-0.5).astype(BF16)
    out[:, width : 2 * width] = grad_keys[...].astype(BF16)
    out[:, 2 * width :] = grad_values[...].astype(BF16)


VMEM = pl.BlockSpec(memory_space=pltpu.VMEM)
SMEM = pl.BlockSpec(memory_space=pltpu.SMEM)


def attention(slopes, proj, seg_col, seg_row):
    length, wide = proj.shape
    width = wide // 3
    heads = width // HEAD
    return pl.pallas_call(
        functools.partial(attention_kernel, block=min(256, length), longest=length // 2),
        out_shape=(
            jax.ShapeDtypeStruct((length, width), BF16),
            jax.ShapeDtypeStruct((heads, length), F32),
        ),
        in_specs=[SMEM, VMEM, VMEM, VMEM],
        out_specs=(VMEM, VMEM),
        compiler_params=pltpu.CompilerParams(vmem_limit_bytes=40 * 2**20),
        cost_estimate=pl.CostEstimate(
            flops=3 * length * length * heads * HEAD, bytes_accessed=4 * length * wide, transcendentals=length * length * heads // 2
        ),
        name="attention",
    )(slopes, proj, seg_col, seg_row)


def attention_back(slopes, proj, grad, seg_col, seg_row, log_total):
    length, wide = proj.shape
    width = wide // 3
    heads = width // HEAD
    block = min(256, length)
    most = min(length, block + length // 2)
    return pl.pallas_call(
        functools.partial(attention_back_kernel, block=block, longest=length // 2),
        out_shape=jax.ShapeDtypeStruct((length, wide), BF16),
        in_specs=[SMEM, VMEM, VMEM, VMEM, VMEM, VMEM],
        out_specs=VMEM,
        scratch_shapes=[
            pltpu.VMEM((most, heads * block), BF16),
            pltpu.VMEM((most, heads * block), BF16),
            pltpu.VMEM((length, width), F32),
            pltpu.VMEM((length, width), F32),
        ],
        compiler_params=pltpu.CompilerParams(vmem_limit_bytes=40 * 2**20),
        cost_estimate=pl.CostEstimate(
            flops=8 * length * length * heads * HEAD, bytes_accessed=6 * length * wide, transcendentals=length * length * heads // 2
        ),
        name="attention_back",
    )(slopes, proj, grad, seg_col, seg_row, log_total)


def copy_kernel(plan, inputs, position, *refs):
    for source, target in plan(position, refs[:inputs], refs[inputs:]):
        target[...] = source[...]


def copy_call(name, plan, position, operands, shapes):
    return pl.pallas_call(
        functools.partial(copy_kernel, plan, len(operands)),
        out_shape=tuple(jax.ShapeDtypeStruct(shape, BF16) for shape in shapes),
        in_specs=[SMEM] + [VMEM] * len(operands),
        out_specs=tuple(VMEM for shape in shapes),
        compiler_params=pltpu.CompilerParams(vmem_limit_bytes=40 * 2**20),
        cost_estimate=pl.CostEstimate(flops=0, bytes_accessed=4 * sum(o.size for o in operands), transcendentals=0),
        name=name,
    )(position, *operands)


def widen_columns_kernel(position, *refs, blocks, rows):
    pieces, out = refs[:-2], refs[-2]
    s = position[0]
    count = len(pieces)
    width = pieces[0].shape[1] // blocks
    for k, piece in enumerate(pieces):
        for j in range(blocks):
            at = pl.multiple_of((j * count + (s ^ k)) * width, width)
            out[:, pl.ds(at, width)] = piece[:rows, j * width : (j + 1) * width].astype(F32)
    refs[-1][...] = tree_sum([piece[rows:, :].astype(F32) for piece in pieces])


def widen_feed_kernel(position, *refs, up_rows, blocks):
    pieces, up, down = refs[:-2], refs[-2], refs[-1]
    s = position[0]
    count = len(pieces)
    width = up.shape[1] // (blocks * count)
    own = down.shape[0] // count
    for k, piece in enumerate(pieces):
        for j in range(blocks):
            at = pl.multiple_of((j * count + (s ^ k)) * width, width)
            up[:, pl.ds(at, width)] = piece[:up_rows, j * width : (j + 1) * width].astype(F32)
        down[pl.ds(pl.multiple_of((s ^ k) * own, own), own), :] = piece[up_rows:, :].astype(F32)


def stats(values):
    center = values - jnp.mean(values, axis=-1, keepdims=True)
    spread = jnp.mean(center * center, axis=-1, keepdims=True)
    rate = lax.rsqrt(spread + EPSILON)
    return center * rate, rate


def norm_back(grad, xhat, rate, gain):
    a = grad * gain
    return rate * (
        a - jnp.mean(a, axis=-1, keepdims=True) - xhat * jnp.mean(a * xhat, axis=-1, keepdims=True)
    )


def tree_sum(terms):
    while len(terms) > 1:
        terms = [a + b for a, b in zip(terms[::2], terms[1::2])]
    return terms[0]


def after(value, *others):
    return lax.optimization_barrier((value, *others))[0]


def body(
    seq_size,
    fsdp_size,
    hidden_in,
    segment_ids,
    ln1_gain,
    ln1_bias,
    w_qkv,
    b_qv,
    w_out,
    b_out,
    ln2_gain,
    ln2_bias,
    w_up,
    b_up,
    w_down,
    b_down,
    cotangent,
):
    S, F, Z = seq_size, fsdp_size, fsdp_size // 2
    s = lax.axis_index("seq")
    f = lax.axis_index("fsdp")
    z, core = f // 2, f % 2

    def seq_x(x, k):
        return lax.ppermute(x, "seq", [(i, i ^ k) for i in range(S)])

    def fsdp_x(x, k):
        return lax.ppermute(x, "fsdp", [(i, i ^ k) for i in range(F)])

    def put(buf, value, *index):
        index = tuple(index) + (0,) * (buf.ndim - len(index))
        return lax.dynamic_update_slice(buf, value, index)

    def spread_fsdp(piece):
        own = [piece] + [fsdp_x(piece, 2 * k) for k in range(1, Z)]
        return own, fsdp_x(jnp.stack(own), 1)

    def join_fsdp(name, pair, heights):
        own, other = pair
        columns = own[0].shape[1]
        ends = [sum(heights[: i + 1]) for i in range(len(heights))]

        def plan(position, ins, outs):
            for k in range(Z):
                for source, place in ((ins[k], 2 * k), (ins[Z].at[k], 2 * k + 1)):
                    for end, height, out in zip(ends, heights, outs):
                        yield source.at[end - height : end, :], out.at[position[1] ^ place]

        return copy_call(
            name, plan, place_now, own + [other], [(F, h, columns) for h in heights]
        )

    def gather_seq_parts(x):
        return [x] + [seq_x(x, k) for k in range(1, S)]

    def exchange_seq(x):
        return lax.all_to_all(x, "seq", 0, 0)

    def reduce_fsdp(partials):
        def half(index):
            return jnp.concatenate(
                [
                    lax.dynamic_index_in_dim(p.reshape(Z, 2, *p.shape[1:]), index, 1, keepdims=False)
                    for p in partials
                ],
                axis=1,
            )

        other = fsdp_x(half(1 - core), 1)
        kept = half(core)

        def block(index):
            return lax.dynamic_index_in_dim(kept, index, 0, keepdims=False).astype(
                F32
            ) + lax.dynamic_index_in_dim(other, index, 0, keepdims=False).astype(F32)

        sent = [fsdp_x(block(z ^ k).astype(BF16), 2 * k) for k in range(1, Z)]
        return sum([x.astype(F32) for x in sent], block(z))

    own_rows = hidden_in.shape[1]
    length = own_rows * S
    width = D // S
    heads = width // HEAD
    part = D // F
    ff_part = b_up.shape[0]
    ff_own = ff_part // S
    hidden = hidden_in[0]
    top = cotangent[0]

    place_now = jnp.stack([s, f])
    wide = 3 * width
    small = jnp.concatenate(
        [ln1_gain, ln1_bias, b_qv[0], b_qv[1], b_out, ln2_gain, ln2_bias, b_down, b_up]
    )
    small_size = small.shape[0]
    extra = -(-small_size // (16 * wide)) * 16
    small_rows = jnp.pad(small, (0, extra * wide - small_size)).reshape(extra, wide)

    aligned = ff_own % 128 == 0
    up_source = w_up
    if not aligned:
        up_source = lax.dynamic_index_in_dim(
            w_up.reshape(part, F, S, ff_own), s, 2, keepdims=False
        ).reshape(ff_own, D)

    def pack_plan(position, ins, outs):
        at = position[0]
        for j in range(3):
            yield (
                ins[0].at[:, pl.ds(pl.multiple_of(j * D + at * width, width), width)],
                outs[0].at[:part, j * width : (j + 1) * width],
            )
        yield ins[1], outs[0].at[part:, :]
        if aligned:
            for j in range(F):
                yield (
                    ins[2].at[:, pl.ds(pl.multiple_of(j * ff_part + at * ff_own, ff_own), ff_own)],
                    outs[1].at[:part, j * ff_own : (j + 1) * ff_own],
                )
        else:
            yield ins[2], outs[1].at[: up_source.shape[0], :]
        yield (
            ins[3].at[pl.ds(pl.multiple_of(at * ff_own, ff_own), ff_own), :],
            outs[1].at[up_source_rows:, :],
        )

    up_source_rows = part * F * ff_own // D
    qkv_piece, feed_piece = copy_call(
        "pack",
        pack_plan,
        place_now,
        [w_qkv, small_rows, up_source, w_down],
        [(part + extra, wide), (up_source_rows + ff_own, D)],
    )

    docs_row = jnp.pad(segment_ids.astype(BF16), ((0, 15), (0, D - own_rows)))
    packed = jnp.concatenate([hidden, docs_row], axis=0)
    hidden_seen = exchange_seq(jnp.broadcast_to(packed[None], (S, *packed.shape)))
    qkv_pair = spread_fsdp(qkv_piece)
    out_pair = spread_fsdp(after(w_out, *qkv_pair[0]))
    feed_pair = spread_fsdp(after(feed_piece, *out_pair[0]))
    top_parts = gather_seq_parts(after(top, hidden_seen))

    hidden_all = hidden_seen[:, :own_rows].reshape(length, D)
    doc_ids = hidden_seen[:, own_rows, :own_rows].astype(jnp.int32).reshape(1, length)
    doc_col = doc_ids.reshape(length, 1)

    full_qkv, small_all = join_fsdp("join_qkv", qkv_pair, [part, extra])
    full_qkv = full_qkv.reshape(D, wide)
    small_all = small_all.reshape(F, extra * wide)[:, :small_size].astype(F32)
    vectors = [small_all[:, i * part : (i + 1) * part].reshape(D) for i in range(8)]
    gain_one, shift_one, bias_q, bias_v, bias_out, gain_two, shift_two, bias_down = vectors
    bias_up = small_all[:, 8 * part :].reshape(F, S, ff_own)
    bias_up = lax.dynamic_index_in_dim(bias_up, s, 1, keepdims=False).reshape(F * ff_own)

    tokens = hidden.astype(F32)
    xhat_all, unused_rate = stats(hidden_all.astype(F32))
    normed_all = (xhat_all * gain_one + shift_one).astype(BF16)
    own_bias = jnp.concatenate(
        [
            lax.dynamic_slice_in_dim(bias_q, s * width, width),
            jnp.zeros((width,), F32),
            lax.dynamic_slice_in_dim(bias_v, s * width, width),
        ]
    )
    projected = (dot(normed_all, full_qkv) + own_bias).astype(BF16)
    slopes = 2.0 ** (-8.0 * (s * heads + jnp.arange(heads) + 1).astype(F32) / H)
    context, log_total = attention(slopes, projected, doc_col, doc_ids)

    context_seen = exchange_seq(context.reshape(S, own_rows, width))
    gathered = jnp.concatenate([context_seen[k] for k in range(S)], axis=1)
    full_out = join_fsdp("join_out", out_pair, [part])[0].reshape(D, D)
    first_sum = tokens + dot(gathered, full_out) + bias_out
    xhat_two, rate_two = stats(first_sum)
    normed_two = (xhat_two * gain_two + shift_two).astype(BF16)
    normed_two_all = jnp.concatenate(gather_seq_parts(normed_two), axis=0)
    top_all = jnp.concatenate(top_parts, axis=0)
    full_up, full_down = join_fsdp("join_feed", feed_pair, [up_source_rows, ff_own])
    full_up = full_up.reshape(D, F * ff_own)
    full_down = full_down.reshape(F * ff_own, D)
    grad_act = dot(top_all, full_down, NT)
    upward = dot(normed_two_all, full_up) + bias_up
    activated, gelu_back = jax.vjp(lambda u: jax.nn.gelu(u, approximate=True), upward)
    activated = activated.astype(BF16)
    grad_upward = gelu_back(grad_act)[0].astype(BF16)
    grad_normed_two = dot(grad_upward, full_up, NT).astype(BF16)

    def scatter_relative(partial):
        total = partial[:own_rows].astype(F32)
        for k in range(1, S):
            block = partial[k * own_rows : (k + 1) * own_rows].astype(BF16)
            total = total + seq_x(block, k).astype(F32)
        return total

    t_two = scatter_relative(grad_normed_two)
    grad_top = top.astype(F32)
    grad_first = grad_top + norm_back(t_two, xhat_two, rate_two, gain_two)
    grad_attended = grad_first.astype(BF16)
    grad_context = dot(grad_attended, full_out, NT).astype(BF16)
    grad_heads = exchange_seq(
        jnp.stack([grad_context[:, k * width : (k + 1) * width] for k in range(S)])
    ).reshape(length, width)

    def owners(partial, columns):
        return partial.astype(BF16).reshape(F, -1, columns)

    grad_feed = reduce_fsdp(
        [owners(dot(normed_two_all, grad_upward, TN), D), owners(dot(activated, top_all, TN), D)]
    )
    result = first_sum + scatter_relative(dot(activated, full_down)) + bias_down
    output = result.astype(BF16)[None]
    grad_out = reduce_fsdp([owners(dot(gathered, grad_attended, TN), D)])

    grad_projected = attention_back(slopes, projected, grad_heads, doc_col, doc_ids, log_total)
    t_part = dot(grad_projected, full_qkv, NT).astype(BF16)
    t_seen = exchange_seq(t_part.reshape(S, own_rows, D))
    t_one = tree_sum([t_seen[k].astype(F32) for k in range(S)])
    xhat_one, rate_one = stats(tokens)
    grad_input = (grad_first + norm_back(t_one, xhat_one, rate_one, gain_one)).astype(BF16)[None]

    def own_columns(values):
        return put(jnp.zeros((D,), F32), values, s * width).reshape(F, part)

    bias_sums = jnp.sum(grad_projected.astype(F32), axis=0)
    grad_bup = jnp.sum(grad_upward.astype(F32), axis=0).reshape(F, 1, ff_own)
    rows = jnp.concatenate(
        [
            jnp.sum(t_part.astype(F32) * xhat_all, axis=0).reshape(F, part),
            jnp.sum(t_part.astype(F32), axis=0).reshape(F, part),
            own_columns(bias_sums[:width]),
            own_columns(bias_sums[2 * width :]),
            jnp.sum(grad_attended.astype(F32), axis=0).reshape(F, part),
            jnp.sum(t_two * xhat_two, axis=0).reshape(F, part),
            jnp.sum(t_two, axis=0).reshape(F, part),
            jnp.sum(grad_top, axis=0).reshape(F, part),
            put(jnp.zeros((F, S, ff_own), F32), grad_bup, 0, s).reshape(F, ff_part),
        ],
        axis=1,
    )
    rows = jnp.pad(rows, ((0, 0), (0, extra * wide - small_size))).reshape(F, extra, wide)
    grad_qkv = reduce_fsdp(
        [owners(dot(normed_all, grad_projected, TN), wide), rows.astype(BF16)]
    )

    sum_out = tree_sum([p.astype(F32) for p in gather_seq_parts(grad_out.astype(BF16))])
    low = gather_seq_parts(grad_feed.astype(BF16))
    if aligned:
        sum_up, sum_down = pl.pallas_call(
            functools.partial(widen_feed_kernel, up_rows=up_source_rows, blocks=F),
            out_shape=(
                jax.ShapeDtypeStruct((part, F * ff_part), F32),
                jax.ShapeDtypeStruct((ff_part, D), F32),
            ),
            in_specs=[SMEM] + [VMEM] * S,
            out_specs=(VMEM, VMEM),
            compiler_params=pltpu.CompilerParams(vmem_limit_bytes=40 * 2**20),
            name="widen_feed",
        )(place_now, *low)
    else:
        sum_up = jnp.zeros((part, F, S, ff_own), F32)
        sum_down = jnp.zeros((ff_part, D), F32)
        for k in range(S):
            up_k = low[k][:up_source_rows].astype(F32).reshape(part, F, 1, ff_own)
            sum_up = put(sum_up, up_k, 0, 0, s ^ k)
            sum_down = put(sum_down, low[k][up_source_rows:].astype(F32), (s ^ k) * ff_own)
    low = gather_seq_parts(grad_qkv.astype(BF16))
    sum_qkv, mine = pl.pallas_call(
        functools.partial(widen_columns_kernel, blocks=3, rows=part),
        out_shape=(
            jax.ShapeDtypeStruct((part, 3 * D), F32),
            jax.ShapeDtypeStruct((extra, wide), F32),
        ),
        in_specs=[SMEM] + [VMEM] * S,
        out_specs=(VMEM, VMEM),
        compiler_params=pltpu.CompilerParams(vmem_limit_bytes=40 * 2**20),
        name="widen_qkv",
    )(place_now, *low)
    mine = mine.reshape(extra * wide)
    pieces = [mine[i * part : (i + 1) * part] for i in range(8)]

    return (
        output,
        grad_input,
        pieces[0],
        pieces[1],
        sum_qkv,
        jnp.stack([pieces[2], pieces[3]]),
        sum_out,
        pieces[4],
        pieces[5],
        pieces[6],
        sum_up.reshape(part, F * ff_part),
        mine[8 * part : small_size],
        sum_down,
        pieces[7],
    )


def solution(mesh):
    return jax.shard_map(
        functools.partial(body, mesh.shape["seq"], mesh.shape["fsdp"]),
        mesh=mesh,
        in_specs=(
            P("fsdp", "seq", None),
            P("fsdp", "seq"),
            P("fsdp"),
            P("fsdp"),
            P("fsdp", None),
            P(None, "fsdp"),
            P("fsdp", None),
            P("fsdp"),
            P("fsdp"),
            P("fsdp"),
            P("fsdp", None),
            P("fsdp"),
            P("fsdp", None),
            P("fsdp"),
            P("fsdp", "seq", None),
        ),
        out_specs=(
            P("fsdp", "seq", None),
            P("fsdp", "seq", None),
            P("fsdp"),
            P("fsdp"),
            P("fsdp", None),
            P(None, "fsdp"),
            P("fsdp", None),
            P("fsdp"),
            P("fsdp"),
            P("fsdp"),
            P("fsdp", None),
            P("fsdp"),
            P("fsdp", None),
            P("fsdp"),
        ),
        check_vma=False,
    )
```

```python
import functools

import jax
import jax.numpy as jnp
from jax import lax
from jax.experimental import pallas as pl
from jax.experimental.pallas import tpu as pltpu
from jax.sharding import PartitionSpec as P

D = 1024
H = 16
HEAD = D // H
EPSILON = 1e-05
F32 = jnp.float32
BF16 = jnp.bfloat16
NT = (((1,), (1,)), ((), ()))
NN = (((1,), (0,)), ((), ()))
TN = (((0,), (0,)), ((), ()))


def dot(a, b, dims=NN):
    return lax.dot_general(a, b, dims, preferred_element_type=F32)


def key_start(first_query, block, longest):
    return max(0, (first_query - longest + 1) // block * block)


def masked_distance(seg_col, seg_row, k0, nk, q0, bq):
    key_at = lax.broadcasted_iota(jnp.int32, (nk, bq), 0) + k0
    query_at = lax.broadcasted_iota(jnp.int32, (nk, bq), 1) + q0
    ok = (key_at <= query_at) & (seg_col[k0 : k0 + nk, :] == seg_row[:, q0 : q0 + bq])
    return jnp.where(ok, (query_at - key_at).astype(F32), 1e32)


def only_head(values, head):
    lane = lax.broadcasted_iota(jnp.int32, values.shape, 1)
    return jnp.where(lane // HEAD == head, values, jnp.zeros_like(values))


def attention_kernel(slopes, proj, seg_col, seg_row, context, log_total, *, block, longest):
    length = proj.shape[0]
    width = proj.shape[1] // 3
    for q0 in range(0, length, block):
        k0 = key_start(q0, block, longest)
        nk = q0 + block - k0
        far = masked_distance(seg_col, seg_row, k0, nk, q0, block)
        queries = proj[q0 : q0 + block, :width] * BF16(HEAD**-0.5)
        keys = proj[k0 : k0 + nk, width : 2 * width]
        values = proj[k0 : k0 + nk, 2 * width :].T
        parts = []
        for head in range(width // HEAD):
            raw = dot(keys, only_head(queries, head), NT) - slopes[head] * far
            highest = jnp.max(raw, axis=0, keepdims=True)
            weights = jnp.exp(raw - highest)
            total = jnp.sum(weights, axis=0, keepdims=True)
            probs = (weights * (1.0 / total)).astype(BF16)
            log_total[head : head + 1, q0 : q0 + block] = highest + jnp.log(total)
            parts.append(dot(values[head * HEAD : (head + 1) * HEAD, :], probs))
        context[q0 : q0 + block, :] = jnp.concatenate(parts, axis=0).T.astype(BF16)


def attention_back_kernel(
    slopes, proj, grad, seg_col, seg_row, log_total, out, probs_all, scores_all, grad_keys, grad_values, *, block, longest
):
    length = proj.shape[0]
    width = proj.shape[1] // 3
    heads = width // HEAD
    grad_keys[...] = jnp.zeros_like(grad_keys)
    grad_values[...] = jnp.zeros_like(grad_values)
    for q0 in range(0, length, block):
        k0 = key_start(q0, block, longest)
        nk = q0 + block - k0
        far = masked_distance(seg_col, seg_row, k0, nk, q0, block)
        queries = proj[q0 : q0 + block, :width] * BF16(HEAD**-0.5)
        keys = proj[k0 : k0 + nk, width : 2 * width]
        values = proj[k0 : k0 + nk, 2 * width :]
        keys_t = keys.T
        tops = grad[q0 : q0 + block, :]
        parts, query_rows, top_rows = [], [], []
        for head in range(heads):
            query_head = only_head(queries, head)
            top_head = only_head(tops, head)
            query_rows.append(query_head)
            top_rows.append(top_head)
            raw = dot(keys, query_head, NT) - slopes[head] * far
            probs = jnp.exp(raw - log_total[head : head + 1, q0 : q0 + block])
            probs_all[:nk, head * block : (head + 1) * block] = probs.astype(BF16)
            grad_probs = dot(values, top_head, NT)
            row_sum = jnp.sum(probs * grad_probs, axis=0, keepdims=True)
            scores = (probs * (grad_probs - row_sum)).astype(BF16)
            scores_all[:nk, head * block : (head + 1) * block] = scores
            parts.append(dot(keys_t[head * HEAD : (head + 1) * HEAD, :], scores))
        grad_values[k0 : k0 + nk, :] += dot(probs_all[:nk, :], jnp.concatenate(top_rows, axis=0))
        grad_keys[k0 : k0 + nk, :] += dot(scores_all[:nk, :], jnp.concatenate(query_rows, axis=0))
        out[q0 : q0 + block, :width] = (jnp.concatenate(parts, axis=0).T * HEAD**-0.5).astype(BF16)
    out[:, width : 2 * width] = grad_keys[...].astype(BF16)
    out[:, 2 * width :] = grad_values[...].astype(BF16)


VMEM = pl.BlockSpec(memory_space=pltpu.VMEM)
SMEM = pl.BlockSpec(memory_space=pltpu.SMEM)


def attention(slopes, proj, seg_col, seg_row):
    length, wide = proj.shape
    width = wide // 3
    heads = width // HEAD
    return pl.pallas_call(
        functools.partial(attention_kernel, block=min(256, length), longest=length // 2),
        out_shape=(
            jax.ShapeDtypeStruct((length, width), BF16),
            jax.ShapeDtypeStruct((heads, length), F32),
        ),
        in_specs=[SMEM, VMEM, VMEM, VMEM],
        out_specs=(VMEM, VMEM),
        compiler_params=pltpu.CompilerParams(vmem_limit_bytes=40 * 2**20),
        cost_estimate=pl.CostEstimate(
            flops=3 * length * length * heads * HEAD, bytes_accessed=4 * length * wide, transcendentals=length * length * heads // 2
        ),
        name="attention",
    )(slopes, proj, seg_col, seg_row)


def attention_back(slopes, proj, grad, seg_col, seg_row, log_total):
    length, wide = proj.shape
    width = wide // 3
    heads = width // HEAD
    block = min(256, length)
    most = min(length, block + length // 2)
    return pl.pallas_call(
        functools.partial(attention_back_kernel, block=block, longest=length // 2),
        out_shape=jax.ShapeDtypeStruct((length, wide), BF16),
        in_specs=[SMEM, VMEM, VMEM, VMEM, VMEM, VMEM],
        out_specs=VMEM,
        scratch_shapes=[
            pltpu.VMEM((most, heads * block), BF16),
            pltpu.VMEM((most, heads * block), BF16),
            pltpu.VMEM((length, width), F32),
            pltpu.VMEM((length, width), F32),
        ],
        compiler_params=pltpu.CompilerParams(vmem_limit_bytes=40 * 2**20),
        cost_estimate=pl.CostEstimate(
            flops=48 * length * length * heads * HEAD, bytes_accessed=6 * length * wide, transcendentals=0
        ),
        name="attention_back",
    )(slopes, proj, grad, seg_col, seg_row, log_total)


def copy_kernel(plan, inputs, position, *refs):
    for source, target in plan(position, refs[:inputs], refs[inputs:]):
        target[...] = source[...]


def copy_call(name, plan, position, operands, shapes):
    return pl.pallas_call(
        functools.partial(copy_kernel, plan, len(operands)),
        out_shape=tuple(jax.ShapeDtypeStruct(shape, BF16) for shape in shapes),
        in_specs=[SMEM] + [VMEM] * len(operands),
        out_specs=tuple(VMEM for shape in shapes),
        compiler_params=pltpu.CompilerParams(vmem_limit_bytes=40 * 2**20),
        cost_estimate=pl.CostEstimate(flops=0, bytes_accessed=4 * sum(o.size for o in operands), transcendentals=0),
        name=name,
    )(position, *operands)


def widen_columns_kernel(pieces, out, sums, *, blocks, rows):
    count, height, columns = pieces.shape
    width = columns // blocks
    for k in range(count):
        for j in range(blocks):
            at = (j * count + k) * width
            out[:, at : at + width] = pieces[k, :rows, j * width : (j + 1) * width].astype(F32)
    sums[...] = tree_sum([pieces[k, rows:, :].astype(F32) for k in range(count)])


def widen_feed_kernel(pieces, up, down, *, up_rows, blocks):
    count = pieces.shape[0]
    part, wide = up.shape
    width = wide // (blocks * count)
    own = down.shape[0] // count
    for k in range(count):
        values = pieces[k, :up_rows, :].astype(F32).reshape(part, blocks * width)
        for j in range(blocks):
            at = (j * count + k) * width
            up[:, at : at + width] = values[:, j * width : (j + 1) * width]
        down[k * own : (k + 1) * own, :] = pieces[k, up_rows:, :].astype(F32)


def project_kernel(seen, weights, gain, shift, bias, projected, normed, xhat):
    values = seen[: normed.shape[0], :].astype(F32)
    center, unused_rate = stats(values)
    xhat[...] = center.astype(BF16)
    low = (center * gain[...] + shift[...]).astype(BF16)
    normed[...] = low
    projected[...] = (dot(low, weights[...]) + bias[...]).astype(BF16)


def project(seen, weights, gain, shift, bias, rows):
    shards, height, width = seen.shape
    wide = weights.shape[1]

    def whole(shape):
        return pl.BlockSpec(shape, lambda i: (0, 0))

    return pl.pallas_call(
        project_kernel,
        grid=(shards,),
        in_specs=[
            pl.BlockSpec((None, height, width), lambda i: (i, 0, 0)),
            whole((width, wide)),
            whole((1, width)),
            whole((1, width)),
            whole((1, wide)),
        ],
        out_specs=(
            pl.BlockSpec((rows, wide), lambda i: (i, 0)),
            pl.BlockSpec((rows, width), lambda i: (i, 0)),
            pl.BlockSpec((rows, width), lambda i: (i, 0)),
        ),
        out_shape=(
            jax.ShapeDtypeStruct((shards * rows, wide), BF16),
            jax.ShapeDtypeStruct((shards * rows, width), BF16),
            jax.ShapeDtypeStruct((shards * rows, width), BF16),
        ),
        compiler_params=pltpu.CompilerParams(vmem_limit_bytes=40 * 2**20),
        cost_estimate=pl.CostEstimate(
            flops=2 * shards * rows * width * wide, bytes_accessed=8 * shards * rows * width, transcendentals=0
        ),
        name="project",
    )(seen, weights, gain[None], shift[None], bias[None])


def stats(values):
    center = values - jnp.mean(values, axis=-1, keepdims=True)
    spread = jnp.mean(center * center, axis=-1, keepdims=True)
    rate = lax.rsqrt(spread + EPSILON)
    return center * rate, rate


def norm_back(grad, xhat, rate, gain):
    a = grad * gain
    return rate * (
        a - jnp.mean(a, axis=-1, keepdims=True) - xhat * jnp.mean(a * xhat, axis=-1, keepdims=True)
    )


def tree_sum(terms):
    while len(terms) > 1:
        terms = [a + b for a, b in zip(terms[::2], terms[1::2])]
    return terms[0]


def together(*values):
    return lax.optimization_barrier(values)


def body(
    seq_size,
    fsdp_size,
    hidden_in,
    segment_ids,
    ln1_gain,
    ln1_bias,
    w_qkv,
    b_qv,
    w_out,
    b_out,
    ln2_gain,
    ln2_bias,
    w_up,
    b_up,
    w_down,
    b_down,
    cotangent,
):
    S, F, Z = seq_size, fsdp_size, fsdp_size // 2
    s = lax.axis_index("seq")
    f = lax.axis_index("fsdp")
    z, core = f // 2, f % 2

    def fsdp_x(x, k):
        return lax.ppermute(x, "fsdp", [(i, i ^ k) for i in range(F)])

    def put(buf, value, *index):
        index = tuple(index) + (0,) * (buf.ndim - len(index))
        return lax.dynamic_update_slice(buf, value, index)

    def spread_z(piece):
        return [piece] + [fsdp_x(piece, 2 * k) for k in range(1, Z)]

    def spread_core(own):
        return own, fsdp_x(jnp.stack(own), 1)

    def join_fsdp(name, pair, heights):
        own, other = pair
        columns = own[0].shape[1]
        ends = [sum(heights[: i + 1]) for i in range(len(heights))]

        def plan(position, ins, outs):
            for k in range(Z):
                for source, place in ((ins[k], 2 * k), (ins[Z].at[k], 2 * k + 1)):
                    for end, height, out in zip(ends, heights, outs):
                        yield source.at[end - height : end, :], out.at[position[1] ^ place]

        return copy_call(
            name, plan, place_now, own + [other], [(F, h, columns) for h in heights]
        )

    def exchange_seq(x):
        return lax.all_to_all(x, "seq", 0, 0)

    def reduce_core(partials):
        def half(index):
            return jnp.concatenate(
                [
                    lax.dynamic_index_in_dim(p.reshape(Z, 2, *p.shape[1:]), index, 1, keepdims=False)
                    for p in partials
                ],
                axis=1,
            )

        other = fsdp_x(half(1 - core), 1)
        kept = half(core)

        def block(index):
            return lax.dynamic_index_in_dim(kept, index, 0, keepdims=False).astype(
                F32
            ) + lax.dynamic_index_in_dim(other, index, 0, keepdims=False).astype(F32)

        return [block(z ^ k).astype(BF16) for k in range(Z)]

    def reduce_z(blocks):
        return [blocks[0]] + [fsdp_x(blocks[k], 2 * k) for k in range(1, Z)]

    def total(seen):
        return tree_sum([x.astype(F32) for x in seen]).astype(BF16)

    own_rows = hidden_in.shape[1]
    length = own_rows * S
    width = D // S
    heads = width // HEAD
    part = D // F
    ff_part = b_up.shape[0]
    ff_own = ff_part // S
    hidden = hidden_in[0]
    top = cotangent[0]

    place_now = jnp.stack([s, f])
    wide = 3 * width
    tall = ff_part // part
    extra = 16
    small = jnp.concatenate(
        [
            v.reshape(-1, part)
            for v in (ln1_gain, ln1_bias, b_qv, b_out, ln2_gain, ln2_bias, b_down, b_up)
        ],
        axis=0,
    )
    small = jnp.pad(small, ((0, extra - small.shape[0]), (0, wide - part)))

    aligned = ff_own % 128 == 0
    up_rows = part * F * ff_own // D
    up_source = w_up
    if not aligned:
        up_source = lax.dynamic_index_in_dim(
            w_up.reshape(part, F, S, ff_own), s, 2, keepdims=False
        ).reshape(up_rows, D)

    def pack_qkv_plan(position, ins, outs):
        at = position[0]
        for j in range(3):
            yield (
                ins[0].at[:, pl.ds(pl.multiple_of(j * D + at * width, width), width)],
                outs[0].at[:part, j * width : (j + 1) * width],
            )
        yield ins[1], outs[0].at[part:, :]

    def pack_rest_plan(position, ins, outs):
        at = position[0]
        if aligned:
            for j in range(F):
                yield (
                    ins[0].at[:, pl.ds(pl.multiple_of(j * ff_part + at * ff_own, ff_own), ff_own)],
                    outs[0].at[:up_rows, j * ff_own : (j + 1) * ff_own],
                )
        else:
            yield ins[0], outs[0].at[:up_rows, :]
        yield (
            ins[1].at[pl.ds(pl.multiple_of(at * ff_own, ff_own), ff_own), :],
            outs[0].at[up_rows:, :],
        )

    def to_all(x):
        return jnp.broadcast_to(x[None], (S, *x.shape))

    (qkv_piece,) = copy_call(
        "pack_qkv", pack_qkv_plan, place_now, [w_qkv, small], [(part + extra, wide)]
    )
    docs_row = jnp.pad(segment_ids.astype(BF16), ((0, 15), (0, D - own_rows)))
    packed, qkv_piece = together(
        to_all(jnp.concatenate([hidden, docs_row], axis=0)), qkv_piece
    )
    hidden_seen = exchange_seq(packed)
    qkv_own = spread_z(qkv_piece)
    hidden_seen, top = together(hidden_seen, top)
    (rest_piece,) = copy_call(
        "pack_rest",
        pack_rest_plan,
        place_now,
        [up_source, w_down],
        [(up_rows + ff_own, D)],
    )
    top_sent, rest_piece, w_out, *qkv_own = together(to_all(top), rest_piece, w_out, *qkv_own)
    qkv_pair = spread_core(qkv_own)
    full_out = lax.all_gather(w_out, "fsdp", axis=0, tiled=True)
    rest = lax.all_gather(rest_piece, "fsdp", axis=0)
    top_all = exchange_seq(top_sent).reshape(length, D)
    doc_ids = hidden_seen[:, own_rows, :own_rows].astype(jnp.int32).reshape(1, length)
    doc_col = doc_ids.reshape(length, 1)

    full_qkv, small_all = join_fsdp("join_qkv", qkv_pair, [part, extra])
    full_qkv = full_qkv.reshape(D, wide)
    small_all = small_all[:, :, :part].astype(F32)
    vectors = [small_all[:, i].reshape(D) for i in range(8)]
    gain_one, shift_one, bias_q, bias_v, bias_out, gain_two, shift_two, bias_down = vectors
    bias_up = small_all[:, 8 : 8 + tall].reshape(F, S, ff_own)
    bias_up = lax.dynamic_index_in_dim(bias_up, s, 1, keepdims=False).reshape(F * ff_own)

    tokens = hidden.astype(F32)
    own_bias = jnp.concatenate(
        [
            lax.dynamic_slice_in_dim(bias_q, s * width, width),
            jnp.zeros((width,), F32),
            lax.dynamic_slice_in_dim(bias_v, s * width, width),
        ]
    )
    projected, normed_all, xhat_all = project(
        hidden_seen, full_qkv, gain_one, shift_one, own_bias, own_rows
    )
    slopes = 2.0 ** (-8.0 * (s * heads + jnp.arange(heads) + 1).astype(F32) / H)
    context, log_total = attention(slopes, projected, doc_col, doc_ids)

    context, top_all = together(context, top_all)
    context_seen = exchange_seq(context.reshape(S, own_rows, width))
    gathered = jnp.concatenate([context_seen[k] for k in range(S)], axis=1)
    full_up = rest[:, :up_rows].reshape(D, F * ff_own)
    full_down = rest[:, up_rows:].reshape(F * ff_own, D)
    first_sum = tokens + dot(gathered, full_out) + bias_out
    xhat_two, rate_two = stats(first_sum)
    normed_two = (xhat_two * gain_two + shift_two).astype(BF16)
    normed_two_all = exchange_seq(to_all(normed_two)).reshape(length, D)
    grad_act = dot(top_all, full_down, NT)
    upward = dot(normed_two_all, full_up) + bias_up
    activated, gelu_back = jax.vjp(lambda u: jax.nn.gelu(u, approximate=True), upward)
    activated = activated.astype(BF16)
    grad_upward = gelu_back(grad_act)[0].astype(BF16)
    grad_normed_two = dot(grad_upward, full_up, NT).astype(BF16)

    def to_tokens(partial):
        return exchange_seq(partial.astype(BF16).reshape(S, own_rows, D))

    def token_sum(seen):
        return tree_sum([seen[k].astype(F32) for k in range(S)])

    def owners(partial, columns):
        return partial.astype(BF16).reshape(F, -1, columns)

    grad_upward, t_two_sent, activated = together(grad_upward, grad_normed_two, activated)
    t_two_seen = to_tokens(t_two_sent)

    def reduce_owner(partial):
        return lax.psum_scatter(partial.astype(BF16), "fsdp", scatter_dimension=0, tiled=True)

    feed_part = jnp.concatenate(
        [
            owners(dot(normed_two_all, grad_upward, TN).reshape(F * up_rows, D), D),
            owners(dot(activated, top_all, TN), D),
        ],
        axis=1,
    ).reshape(F * (up_rows + ff_own), D)
    result_part = dot(activated, full_down).astype(BF16)
    t_two_seen, feed_part, result_part = together(t_two_seen, feed_part, result_part)
    feed_mine = reduce_owner(feed_part)
    t_two = token_sum(t_two_seen)
    grad_top = top.astype(F32)
    grad_first = grad_top + norm_back(t_two, xhat_two, rate_two, gain_two)
    grad_attended = grad_first.astype(BF16)
    grad_context = dot(grad_attended, full_out, NT).astype(BF16)
    grad_heads = exchange_seq(
        jnp.stack([grad_context[:, k * width : (k + 1) * width] for k in range(S)])
    ).reshape(length, width)

    out_part = dot(gathered, grad_attended, TN).astype(BF16)
    grad_heads, result_part, out_part = together(grad_heads, result_part, out_part)
    out_mine = reduce_owner(out_part)
    result_seen = to_tokens(result_part)
    grad_projected = attention_back(slopes, projected, grad_heads, doc_col, doc_ids, log_total)
    t_part = dot(grad_projected, full_qkv, NT).astype(BF16)
    t_part, grad_projected, result_seen = together(t_part, grad_projected, result_seen)
    t_one_seen = to_tokens(t_part)
    output = (first_sum + token_sum(result_seen) + bias_down).astype(BF16)[None]

    def own_columns(values):
        return put(jnp.zeros((D,), F32), values, s * width)

    bias_sums = jnp.sum(grad_projected.astype(F32), axis=0)
    grad_bup = jnp.sum(grad_upward.astype(F32), axis=0).reshape(F, 1, ff_own)
    low_t = t_part.astype(F32)
    rows = jnp.stack(
        [
            v.reshape(F, part)
            for v in (
                jnp.sum(low_t * xhat_all.astype(F32), axis=0),
                jnp.sum(low_t, axis=0),
                own_columns(bias_sums[:width]),
                own_columns(bias_sums[2 * width :]),
                jnp.sum(grad_attended.astype(F32), axis=0),
                jnp.sum(t_two * xhat_two, axis=0),
                jnp.sum(t_two, axis=0),
                jnp.sum(grad_top, axis=0),
            )
        ],
        axis=1,
    )
    bup_rows = put(jnp.zeros((F, S, ff_own), F32), grad_bup, 0, s).reshape(F, tall, part)
    rows = jnp.concatenate([rows, bup_rows], axis=1)
    rows = jnp.pad(rows, ((0, 0), (0, extra - rows.shape[1]), (0, wide - part))).astype(BF16)
    qkv_blocks = reduce_core([owners(dot(normed_all, grad_projected, TN), wide), rows])
    qkv_sent = reduce_z(qkv_blocks)
    t_one_seen, feed_sent, *unused_blocks = together(t_one_seen, to_all(feed_mine), *qkv_blocks)
    t_one = token_sum(t_one_seen)
    xhat_one, rate_one = stats(tokens)
    grad_input = (grad_first + norm_back(t_one, xhat_one, rate_one, gain_one)).astype(BF16)[None]


    feed_seen = exchange_seq(feed_sent)
    feed_seen, out_mine, *qkv_sent = together(feed_seen, out_mine, *qkv_sent)
    sum_up, sum_down = pl.pallas_call(
        functools.partial(widen_feed_kernel, up_rows=up_rows, blocks=F),
        out_shape=(
            jax.ShapeDtypeStruct((part, F * ff_part), F32),
            jax.ShapeDtypeStruct((ff_part, D), F32),
        ),
        in_specs=[VMEM],
        out_specs=(VMEM, VMEM),
        compiler_params=pltpu.CompilerParams(vmem_limit_bytes=40 * 2**20),
        name="widen_feed",
    )(feed_seen)
    out_seen = exchange_seq(to_all(out_mine))
    sum_out = tree_sum([out_seen[k].astype(F32) for k in range(S)])
    qkv_seen = exchange_seq(to_all(total(qkv_sent)))
    sum_qkv, mine = pl.pallas_call(
        functools.partial(widen_columns_kernel, blocks=3, rows=part),
        out_shape=(
            jax.ShapeDtypeStruct((part, 3 * D), F32),
            jax.ShapeDtypeStruct((extra, wide), F32),
        ),
        in_specs=[VMEM],
        out_specs=(VMEM, VMEM),
        compiler_params=pltpu.CompilerParams(vmem_limit_bytes=40 * 2**20),
        name="widen_qkv",
    )(qkv_seen)
    pieces = [mine[i, :part] for i in range(8)]

    return (
        output,
        grad_input,
        pieces[0],
        pieces[1],
        sum_qkv,
        jnp.stack([pieces[2], pieces[3]]),
        sum_out,
        pieces[4],
        pieces[5],
        pieces[6],
        sum_up.reshape(part, F * ff_part),
        mine[8 : 8 + tall, :part].reshape(ff_part),
        sum_down,
        pieces[7],
    )


def solution(mesh):
    return jax.shard_map(
        functools.partial(body, mesh.shape["seq"], mesh.shape["fsdp"]),
        mesh=mesh,
        in_specs=(
            P("fsdp", "seq", None),
            P("fsdp", "seq"),
            P("fsdp"),
            P("fsdp"),
            P("fsdp", None),
            P(None, "fsdp"),
            P("fsdp", None),
            P("fsdp"),
            P("fsdp"),
            P("fsdp"),
            P("fsdp", None),
            P("fsdp"),
            P("fsdp", None),
            P("fsdp"),
            P("fsdp", "seq", None),
        ),
        out_specs=(
            P("fsdp", "seq", None),
            P("fsdp", "seq", None),
            P("fsdp"),
            P("fsdp"),
            P("fsdp", None),
            P(None, "fsdp"),
            P("fsdp", None),
            P("fsdp"),
            P("fsdp"),
            P("fsdp"),
            P("fsdp", None),
            P("fsdp"),
            P("fsdp", None),
            P("fsdp"),
        ),
        check_vma=False,
    )
```

```python
import functools

import jax
import jax.numpy as jnp
from jax import lax
from jax.experimental import pallas as pl
from jax.experimental.pallas import tpu as pltpu
from jax.sharding import PartitionSpec as P

D = 1024
H = 16
HEAD = D // H
EPSILON = 1e-05
F32 = jnp.float32
BF16 = jnp.bfloat16
NT = (((1,), (1,)), ((), ()))
NN = (((1,), (0,)), ((), ()))
TN = (((0,), (0,)), ((), ()))


def dot(a, b, dims=NN):
    return lax.dot_general(a, b, dims, preferred_element_type=F32)


def key_start(first_query, block, longest):
    return max(0, (first_query - longest + 1) // block * block)


def masked_distance(seg_col, seg_row, k0, nk, q0, bq):
    key_at = lax.broadcasted_iota(jnp.int32, (nk, bq), 0) + k0
    query_at = lax.broadcasted_iota(jnp.int32, (nk, bq), 1) + q0
    ok = (key_at <= query_at) & (seg_col[k0 : k0 + nk, :] == seg_row[:, q0 : q0 + bq])
    return jnp.where(ok, (query_at - key_at).astype(F32), 1e32)


def only_head(values, head):
    lane = lax.broadcasted_iota(jnp.int32, values.shape, 1)
    return jnp.where(lane // HEAD == head, values, jnp.zeros_like(values))


def attention_kernel(slopes, proj, seg_col, seg_row, context, log_total, *, block, longest):
    length = proj.shape[0]
    width = proj.shape[1] // 3
    for q0 in range(0, length, block):
        k0 = key_start(q0, block, longest)
        nk = q0 + block - k0
        far = masked_distance(seg_col, seg_row, k0, nk, q0, block)
        queries = proj[q0 : q0 + block, :width] * BF16(HEAD**-0.5)
        keys = proj[k0 : k0 + nk, width : 2 * width]
        values = proj[k0 : k0 + nk, 2 * width :].T
        parts = []
        for head in range(width // HEAD):
            raw = dot(keys, only_head(queries, head), NT) - slopes[head] * far
            highest = jnp.max(raw, axis=0, keepdims=True)
            weights = jnp.exp(raw - highest)
            total = jnp.sum(weights, axis=0, keepdims=True)
            probs = (weights * (1.0 / total)).astype(BF16)
            log_total[head : head + 1, q0 : q0 + block] = highest + jnp.log(total)
            parts.append(dot(values[head * HEAD : (head + 1) * HEAD, :], probs))
        context[q0 : q0 + block, :] = jnp.concatenate(parts, axis=0).T.astype(BF16)


def attention_back_kernel(
    slopes, proj, grad, seg_col, seg_row, log_total, out, probs_all, scores_all, grad_keys, grad_values, *, block, longest
):
    length = proj.shape[0]
    width = proj.shape[1] // 3
    heads = width // HEAD
    grad_keys[...] = jnp.zeros_like(grad_keys)
    grad_values[...] = jnp.zeros_like(grad_values)
    for q0 in range(0, length, block):
        k0 = key_start(q0, block, longest)
        nk = q0 + block - k0
        far = masked_distance(seg_col, seg_row, k0, nk, q0, block)
        queries = proj[q0 : q0 + block, :width] * BF16(HEAD**-0.5)
        keys = proj[k0 : k0 + nk, width : 2 * width]
        values = proj[k0 : k0 + nk, 2 * width :]
        keys_t = keys.T
        tops = grad[q0 : q0 + block, :]
        parts, query_rows, top_rows = [], [], []
        for head in range(heads):
            query_head = only_head(queries, head)
            top_head = only_head(tops, head)
            query_rows.append(query_head)
            top_rows.append(top_head)
            raw = dot(keys, query_head, NT) - slopes[head] * far
            probs = jnp.exp(raw - log_total[head : head + 1, q0 : q0 + block])
            probs_all[:nk, head * block : (head + 1) * block] = probs.astype(BF16)
            grad_probs = dot(values, top_head, NT)
            row_sum = jnp.sum(probs * grad_probs, axis=0, keepdims=True)
            scores = (probs * (grad_probs - row_sum)).astype(BF16)
            scores_all[:nk, head * block : (head + 1) * block] = scores
            parts.append(dot(keys_t[head * HEAD : (head + 1) * HEAD, :], scores))
        grad_values[k0 : k0 + nk, :] += dot(probs_all[:nk, :], jnp.concatenate(top_rows, axis=0))
        grad_keys[k0 : k0 + nk, :] += dot(scores_all[:nk, :], jnp.concatenate(query_rows, axis=0))
        out[q0 : q0 + block, :width] = (jnp.concatenate(parts, axis=0).T * HEAD**-0.5).astype(BF16)
    out[:, width : 2 * width] = grad_keys[...].astype(BF16)
    out[:, 2 * width :] = grad_values[...].astype(BF16)


VMEM = pl.BlockSpec(memory_space=pltpu.VMEM)
SMEM = pl.BlockSpec(memory_space=pltpu.SMEM)


def attention(slopes, proj, seg_col, seg_row):
    length, wide = proj.shape
    width = wide // 3
    heads = width // HEAD
    return pl.pallas_call(
        functools.partial(attention_kernel, block=min(256, length), longest=length // 2),
        out_shape=(
            jax.ShapeDtypeStruct((length, width), BF16),
            jax.ShapeDtypeStruct((heads, length), F32),
        ),
        in_specs=[SMEM, VMEM, VMEM, VMEM],
        out_specs=(VMEM, VMEM),
        compiler_params=pltpu.CompilerParams(vmem_limit_bytes=40 * 2**20),
        cost_estimate=pl.CostEstimate(
            flops=3 * length * length * heads * HEAD, bytes_accessed=4 * length * wide, transcendentals=length * length * heads // 2
        ),
        name="attention",
    )(slopes, proj, seg_col, seg_row)


def attention_back(slopes, proj, grad, seg_col, seg_row, log_total):
    length, wide = proj.shape
    width = wide // 3
    heads = width // HEAD
    block = min(256, length)
    most = min(length, block + length // 2)
    return pl.pallas_call(
        functools.partial(attention_back_kernel, block=block, longest=length // 2),
        out_shape=jax.ShapeDtypeStruct((length, wide), BF16),
        in_specs=[SMEM, VMEM, VMEM, VMEM, VMEM, VMEM],
        out_specs=VMEM,
        scratch_shapes=[
            pltpu.VMEM((most, heads * block), BF16),
            pltpu.VMEM((most, heads * block), BF16),
            pltpu.VMEM((length, width), F32),
            pltpu.VMEM((length, width), F32),
        ],
        compiler_params=pltpu.CompilerParams(vmem_limit_bytes=40 * 2**20),
        cost_estimate=pl.CostEstimate(
            flops=48 * length * length * heads * HEAD, bytes_accessed=6 * length * wide, transcendentals=0
        ),
        name="attention_back",
    )(slopes, proj, grad, seg_col, seg_row, log_total)


def copy_kernel(plan, inputs, position, *refs):
    for source, target in plan(position, refs[:inputs], refs[inputs:]):
        target[...] = source[...]


def copy_call(name, plan, position, operands, shapes):
    return pl.pallas_call(
        functools.partial(copy_kernel, plan, len(operands)),
        out_shape=tuple(jax.ShapeDtypeStruct(shape, BF16) for shape in shapes),
        in_specs=[SMEM] + [VMEM] * len(operands),
        out_specs=tuple(VMEM for shape in shapes),
        compiler_params=pltpu.CompilerParams(vmem_limit_bytes=40 * 2**20),
        cost_estimate=pl.CostEstimate(flops=0, bytes_accessed=4 * sum(o.size for o in operands), transcendentals=0),
        name=name,
    )(position, *operands)


def widen_columns_kernel(pieces, out, sums, *, blocks, rows):
    count, height, columns = pieces.shape
    width = columns // blocks
    for k in range(count):
        for j in range(blocks):
            at = (j * count + k) * width
            out[:, at : at + width] = pieces[k, :rows, j * width : (j + 1) * width].astype(F32)
    sums[...] = tree_sum([pieces[k, rows:, :].astype(F32) for k in range(count)])


def widen_feed_kernel(pieces, up, down, *, up_rows, blocks):
    count = pieces.shape[0]
    part, wide = up.shape
    width = wide // (blocks * count)
    own = down.shape[0] // count
    for k in range(count):
        values = pieces[k, :up_rows, :].astype(F32).reshape(part, blocks * width)
        for j in range(blocks):
            at = (j * count + k) * width
            up[:, at : at + width] = values[:, j * width : (j + 1) * width]
        down[k * own : (k + 1) * own, :] = pieces[k, up_rows:, :].astype(F32)


def project_kernel(seen, weights, gain, shift, bias, projected, normed, xhat):
    values = seen[: normed.shape[0], :].astype(F32)
    center, unused_rate = stats(values)
    xhat[...] = center.astype(BF16)
    low = (center * gain[...] + shift[...]).astype(BF16)
    normed[...] = low
    projected[...] = (dot(low, weights[...]) + bias[...]).astype(BF16)


def project(seen, weights, gain, shift, bias, rows):
    shards, height, width = seen.shape
    wide = weights.shape[1]

    def whole(shape):
        return pl.BlockSpec(shape, lambda i: (0, 0))

    return pl.pallas_call(
        project_kernel,
        grid=(shards,),
        in_specs=[
            pl.BlockSpec((None, height, width), lambda i: (i, 0, 0)),
            whole((width, wide)),
            whole((1, width)),
            whole((1, width)),
            whole((1, wide)),
        ],
        out_specs=(
            pl.BlockSpec((rows, wide), lambda i: (i, 0)),
            pl.BlockSpec((rows, width), lambda i: (i, 0)),
            pl.BlockSpec((rows, width), lambda i: (i, 0)),
        ),
        out_shape=(
            jax.ShapeDtypeStruct((shards * rows, wide), BF16),
            jax.ShapeDtypeStruct((shards * rows, width), BF16),
            jax.ShapeDtypeStruct((shards * rows, width), BF16),
        ),
        compiler_params=pltpu.CompilerParams(vmem_limit_bytes=40 * 2**20),
        cost_estimate=pl.CostEstimate(
            flops=2 * shards * rows * width * wide, bytes_accessed=8 * shards * rows * width, transcendentals=0
        ),
        name="project",
    )(seen, weights, gain[None], shift[None], bias[None])


def feed_kernel(normed, top, up, down, bias, activated, grad_upward, back, bias_sum):
    weights = up[...].reshape(normed.shape[1], -1)
    upward = dot(normed[...], weights) + bias[...]
    grad_act = dot(top[...], down[...].reshape(-1, top.shape[1]), NT)
    square = upward * upward
    slope = 0.7978845608028654
    bend = jnp.tanh(slope * upward * (1.0 + 0.044715 * square))
    half = 0.5 * (1.0 + bend)
    activated[...] = (upward * half).astype(BF16)
    rise = half + 0.5 * slope * upward * (1.0 - bend * bend) * (1.0 + 0.134145 * square)
    low = (grad_act * rise).astype(BF16)
    grad_upward[...] = low
    back[...] = dot(low, weights, NT).astype(BF16)

    @pl.when(pl.program_id(0) == 0)
    def clear():
        bias_sum[...] = jnp.zeros_like(bias_sum)

    bias_sum[...] += jnp.sum(low.astype(F32), axis=0, keepdims=True)


def feed_forward(normed, top, up, down, up_shape, down_shape, down_place, bias):
    length, width = normed.shape
    rows = min(256, length)
    hidden = bias.shape[0]

    def part(columns):
        return pl.BlockSpec((rows, columns), lambda i: (i, 0))

    return pl.pallas_call(
        feed_kernel,
        grid=(length // rows,),
        in_specs=[
            part(width),
            part(width),
            pl.BlockSpec(up_shape, lambda i: (0, 0, 0)),
            pl.BlockSpec(down_shape, lambda i: (0, down_place, 0)),
            pl.BlockSpec((1, hidden), lambda i: (0, 0)),
        ],
        out_specs=(
            part(hidden),
            part(hidden),
            part(width),
            pl.BlockSpec((1, hidden), lambda i: (0, 0)),
        ),
        out_shape=(
            jax.ShapeDtypeStruct((length, hidden), BF16),
            jax.ShapeDtypeStruct((length, hidden), BF16),
            jax.ShapeDtypeStruct((length, width), BF16),
            jax.ShapeDtypeStruct((1, hidden), F32),
        ),
        compiler_params=pltpu.CompilerParams(vmem_limit_bytes=48 * 2**20),
        cost_estimate=pl.CostEstimate(
            flops=6 * length * width * hidden, bytes_accessed=12 * length * width, transcendentals=length * hidden
        ),
        name="feed_forward",
    )(normed, top, up, down, bias[None])


def stats(values):
    center = values - jnp.mean(values, axis=-1, keepdims=True)
    spread = jnp.mean(center * center, axis=-1, keepdims=True)
    rate = lax.rsqrt(spread + EPSILON)
    return center * rate, rate


def norm_back(grad, xhat, rate, gain):
    a = grad * gain
    return rate * (
        a - jnp.mean(a, axis=-1, keepdims=True) - xhat * jnp.mean(a * xhat, axis=-1, keepdims=True)
    )


def tree_sum(terms):
    while len(terms) > 1:
        terms = [a + b for a, b in zip(terms[::2], terms[1::2])]
    return terms[0]


def together(*values):
    return lax.optimization_barrier(values)


def body(
    seq_size,
    fsdp_size,
    hidden_in,
    segment_ids,
    ln1_gain,
    ln1_bias,
    w_qkv,
    b_qv,
    w_out,
    b_out,
    ln2_gain,
    ln2_bias,
    w_up,
    b_up,
    w_down,
    b_down,
    cotangent,
):
    S, F, Z = seq_size, fsdp_size, fsdp_size // 2
    s = lax.axis_index("seq")
    f = lax.axis_index("fsdp")
    z, core = f // 2, f % 2

    def fsdp_x(x, k):
        return lax.ppermute(x, "fsdp", [(i, i ^ k) for i in range(F)])

    def put(buf, value, *index):
        index = tuple(index) + (0,) * (buf.ndim - len(index))
        return lax.dynamic_update_slice(buf, value, index)

    def spread_z(piece):
        return [piece] + [fsdp_x(piece, 2 * k) for k in range(1, Z)]

    def spread_core(own):
        return own, fsdp_x(jnp.stack(own), 1)

    def join_fsdp(name, pair, heights):
        own, other = pair
        columns = own[0].shape[1]
        ends = [sum(heights[: i + 1]) for i in range(len(heights))]

        def plan(position, ins, outs):
            for k in range(Z):
                for source, place in ((ins[k], 2 * k), (ins[Z].at[k], 2 * k + 1)):
                    for end, height, out in zip(ends, heights, outs):
                        yield source.at[end - height : end, :], out.at[position[1] ^ place]

        return copy_call(
            name, plan, place_now, own + [other], [(F, h, columns) for h in heights]
        )

    def exchange_seq(x):
        return lax.all_to_all(x, "seq", 0, 0)

    def reduce_core(partials):
        def half(index):
            return jnp.concatenate(
                [
                    lax.dynamic_index_in_dim(p.reshape(Z, 2, *p.shape[1:]), index, 1, keepdims=False)
                    for p in partials
                ],
                axis=1,
            )

        other = fsdp_x(half(1 - core), 1)
        kept = half(core)

        def block(index):
            return lax.dynamic_index_in_dim(kept, index, 0, keepdims=False).astype(
                F32
            ) + lax.dynamic_index_in_dim(other, index, 0, keepdims=False).astype(F32)

        return [block(z ^ k).astype(BF16) for k in range(Z)]

    def reduce_z(blocks):
        return [blocks[0]] + [fsdp_x(blocks[k], 2 * k) for k in range(1, Z)]

    def total(seen):
        return tree_sum([x.astype(F32) for x in seen]).astype(BF16)

    own_rows = hidden_in.shape[1]
    length = own_rows * S
    width = D // S
    heads = width // HEAD
    part = D // F
    ff_part = b_up.shape[0]
    ff_own = ff_part // S
    hidden = hidden_in[0]
    top = cotangent[0]

    place_now = jnp.stack([s, f])
    wide = 3 * width
    tall = ff_part // part
    extra = 16
    small = jnp.concatenate(
        [
            v.reshape(-1, part)
            for v in (ln1_gain, ln1_bias, b_qv, b_out, ln2_gain, ln2_bias, b_down, b_up)
        ],
        axis=0,
    )
    small = jnp.pad(small, ((0, extra - small.shape[0]), (0, wide - part)))

    aligned = ff_own % 128 == 0
    up_rows = part * F * ff_own // D
    up_source = w_up
    if not aligned:
        up_source = lax.dynamic_index_in_dim(
            w_up.reshape(part, F, S, ff_own), s, 2, keepdims=False
        ).reshape(up_rows, D)

    def pack_qkv_plan(position, ins, outs):
        at = position[0]
        for j in range(3):
            yield (
                ins[0].at[:, pl.ds(pl.multiple_of(j * D + at * width, width), width)],
                outs[0].at[:part, j * width : (j + 1) * width],
            )
        yield ins[1], outs[0].at[part:, :]

    def pack_rest_plan(position, ins, outs):
        at = position[0]
        if aligned:
            for j in range(F):
                yield (
                    ins[0].at[:, pl.ds(pl.multiple_of(j * ff_part + at * ff_own, ff_own), ff_own)],
                    outs[0].at[:up_rows, j * ff_own : (j + 1) * ff_own],
                )
        else:
            yield ins[0], outs[0].at[:up_rows, :]
        yield (
            ins[1].at[pl.ds(pl.multiple_of(at * ff_own, ff_own), ff_own), :],
            outs[0].at[up_rows:, :],
        )

    def to_all(x):
        return jnp.broadcast_to(x[None], (S, *x.shape))

    (qkv_piece,) = copy_call(
        "pack_qkv", pack_qkv_plan, place_now, [w_qkv, small], [(part + extra, wide)]
    )
    docs_row = jnp.pad(segment_ids.astype(BF16), ((0, 15), (0, D - own_rows)))
    packed, qkv_piece = together(
        to_all(jnp.concatenate([hidden, docs_row], axis=0)), qkv_piece
    )
    hidden_seen = exchange_seq(packed)
    qkv_own = spread_z(qkv_piece)
    hidden_seen, top = together(hidden_seen, top)
    (rest_piece,) = copy_call(
        "pack_rest",
        pack_rest_plan,
        place_now,
        [up_source, w_down],
        [(up_rows + ff_own, D)],
    )
    top_sent, rest_piece, w_out, *qkv_own = together(to_all(top), rest_piece, w_out, *qkv_own)
    qkv_pair = spread_core(qkv_own)
    full_out = lax.all_gather(w_out, "fsdp", axis=0, tiled=True)
    rest = lax.all_gather(rest_piece, "fsdp", axis=0)
    top_all = exchange_seq(top_sent).reshape(length, D)
    doc_ids = hidden_seen[:, own_rows, :own_rows].astype(jnp.int32).reshape(1, length)
    doc_col = doc_ids.reshape(length, 1)

    full_qkv, small_all = join_fsdp("join_qkv", qkv_pair, [part, extra])
    full_qkv = full_qkv.reshape(D, wide)
    small_all = small_all[:, :, :part].astype(F32)
    vectors = [small_all[:, i].reshape(D) for i in range(8)]
    gain_one, shift_one, bias_q, bias_v, bias_out, gain_two, shift_two, bias_down = vectors
    bias_up = small_all[:, 8 : 8 + tall].reshape(F, S, ff_own)
    bias_up = lax.dynamic_index_in_dim(bias_up, s, 1, keepdims=False).reshape(F * ff_own)

    tokens = hidden.astype(F32)
    own_bias = jnp.concatenate(
        [
            lax.dynamic_slice_in_dim(bias_q, s * width, width),
            jnp.zeros((width,), F32),
            lax.dynamic_slice_in_dim(bias_v, s * width, width),
        ]
    )
    projected, normed_all, xhat_all = project(
        hidden_seen, full_qkv, gain_one, shift_one, own_bias, own_rows
    )
    slopes = 2.0 ** (-8.0 * (s * heads + jnp.arange(heads) + 1).astype(F32) / H)
    context, log_total = attention(slopes, projected, doc_col, doc_ids)

    context, top_all = together(context, top_all)
    context_seen = exchange_seq(context.reshape(S, own_rows, width))
    gathered = jnp.concatenate([context_seen[k] for k in range(S)], axis=1)
    full_up = rest[:, :up_rows].reshape(D, F * ff_own)
    full_down = rest[:, up_rows:].reshape(F * ff_own, D)
    first_sum = tokens + dot(gathered, full_out) + bias_out
    xhat_two, rate_two = stats(first_sum)
    normed_two = (xhat_two * gain_two + shift_two).astype(BF16)
    normed_two_all = exchange_seq(to_all(normed_two)).reshape(length, D)
    if F * ff_own == D and up_rows == ff_own:
        feed_weights = (rest, rest, (F, part, D), (F, ff_own, D), 1)
    else:
        feed_weights = (
            full_up.reshape(F, part, F * ff_own),
            full_down.reshape(F, ff_own, D),
            (F, part, F * ff_own),
            (F, ff_own, D),
            0,
        )
    activated, grad_upward, grad_normed_two, bias_up_sum = feed_forward(
        normed_two_all, top_all, *feed_weights, bias_up
    )

    def to_tokens(partial):
        return exchange_seq(partial.astype(BF16).reshape(S, own_rows, D))

    def token_sum(seen):
        return tree_sum([seen[k].astype(F32) for k in range(S)])

    def owners(partial, columns):
        return partial.astype(BF16).reshape(F, -1, columns)

    grad_upward, t_two_sent, activated = together(grad_upward, grad_normed_two, activated)
    t_two_seen = to_tokens(t_two_sent)

    def reduce_owner(partial):
        return lax.psum_scatter(partial.astype(BF16), "fsdp", scatter_dimension=0, tiled=True)

    feed_part = jnp.concatenate(
        [
            owners(dot(normed_two_all, grad_upward, TN).reshape(F * up_rows, D), D),
            owners(dot(activated, top_all, TN), D),
        ],
        axis=1,
    ).reshape(F * (up_rows + ff_own), D)
    result_part = dot(activated, full_down).astype(BF16)
    t_two_seen, feed_part, result_part = together(t_two_seen, feed_part, result_part)
    feed_mine = reduce_owner(feed_part)
    t_two = token_sum(t_two_seen)
    grad_top = top.astype(F32)
    grad_first = grad_top + norm_back(t_two, xhat_two, rate_two, gain_two)
    grad_attended = grad_first.astype(BF16)
    grad_context = dot(grad_attended, full_out, NT).astype(BF16)
    grad_heads = exchange_seq(
        jnp.stack([grad_context[:, k * width : (k + 1) * width] for k in range(S)])
    ).reshape(length, width)

    out_part = dot(gathered, grad_attended, TN).astype(BF16)
    grad_heads, result_part, out_part = together(grad_heads, result_part, out_part)
    out_mine = reduce_owner(out_part)
    result_seen = to_tokens(result_part)
    grad_projected = attention_back(slopes, projected, grad_heads, doc_col, doc_ids, log_total)
    t_part = dot(grad_projected, full_qkv, NT).astype(BF16)
    t_part, grad_projected, result_seen = together(t_part, grad_projected, result_seen)
    t_one_seen = to_tokens(t_part)
    output = (first_sum + token_sum(result_seen) + bias_down).astype(BF16)[None]

    def own_columns(values):
        return put(jnp.zeros((D,), F32), values, s * width)

    bias_sums = jnp.sum(grad_projected.astype(F32), axis=0)
    grad_bup = bias_up_sum.reshape(F, 1, ff_own)
    low_t = t_part.astype(F32)
    rows = jnp.stack(
        [
            v.reshape(F, part)
            for v in (
                jnp.sum(low_t * xhat_all.astype(F32), axis=0),
                jnp.sum(low_t, axis=0),
                own_columns(bias_sums[:width]),
                own_columns(bias_sums[2 * width :]),
                jnp.sum(grad_attended.astype(F32), axis=0),
                jnp.sum(t_two * xhat_two, axis=0),
                jnp.sum(t_two, axis=0),
                jnp.sum(grad_top, axis=0),
            )
        ],
        axis=1,
    )
    bup_rows = put(jnp.zeros((F, S, ff_own), F32), grad_bup, 0, s).reshape(F, tall, part)
    rows = jnp.concatenate([rows, bup_rows], axis=1)
    rows = jnp.pad(rows, ((0, 0), (0, extra - rows.shape[1]), (0, wide - part))).astype(BF16)
    qkv_blocks = reduce_core([owners(dot(normed_all, grad_projected, TN), wide), rows])
    qkv_sent = reduce_z(qkv_blocks)
    t_one_seen, feed_sent, *unused_blocks = together(t_one_seen, to_all(feed_mine), *qkv_blocks)
    t_one = token_sum(t_one_seen)
    xhat_one, rate_one = stats(tokens)
    grad_input = (grad_first + norm_back(t_one, xhat_one, rate_one, gain_one)).astype(BF16)[None]


    feed_seen = exchange_seq(feed_sent)
    feed_seen, out_mine, *qkv_sent = together(feed_seen, out_mine, *qkv_sent)
    sum_up, sum_down = pl.pallas_call(
        functools.partial(widen_feed_kernel, up_rows=up_rows, blocks=F),
        out_shape=(
            jax.ShapeDtypeStruct((part, F * ff_part), F32),
            jax.ShapeDtypeStruct((ff_part, D), F32),
        ),
        in_specs=[VMEM],
        out_specs=(VMEM, VMEM),
        compiler_params=pltpu.CompilerParams(vmem_limit_bytes=40 * 2**20),
        name="widen_feed",
    )(feed_seen)
    out_seen = exchange_seq(to_all(out_mine))
    sum_out = tree_sum([out_seen[k].astype(F32) for k in range(S)])
    qkv_seen = exchange_seq(to_all(total(qkv_sent)))
    sum_qkv, mine = pl.pallas_call(
        functools.partial(widen_columns_kernel, blocks=3, rows=part),
        out_shape=(
            jax.ShapeDtypeStruct((part, 3 * D), F32),
            jax.ShapeDtypeStruct((extra, wide), F32),
        ),
        in_specs=[VMEM],
        out_specs=(VMEM, VMEM),
        compiler_params=pltpu.CompilerParams(vmem_limit_bytes=40 * 2**20),
        name="widen_qkv",
    )(qkv_seen)
    pieces = [mine[i, :part] for i in range(8)]

    return (
        output,
        grad_input,
        pieces[0],
        pieces[1],
        sum_qkv,
        jnp.stack([pieces[2], pieces[3]]),
        sum_out,
        pieces[4],
        pieces[5],
        pieces[6],
        sum_up.reshape(part, F * ff_part),
        mine[8 : 8 + tall, :part].reshape(ff_part),
        sum_down,
        pieces[7],
    )


def solution(mesh):
    return jax.shard_map(
        functools.partial(body, mesh.shape["seq"], mesh.shape["fsdp"]),
        mesh=mesh,
        in_specs=(
            P("fsdp", "seq", None),
            P("fsdp", "seq"),
            P("fsdp"),
            P("fsdp"),
            P("fsdp", None),
            P(None, "fsdp"),
            P("fsdp", None),
            P("fsdp"),
            P("fsdp"),
            P("fsdp"),
            P("fsdp", None),
            P("fsdp"),
            P("fsdp", None),
            P("fsdp"),
            P("fsdp", "seq", None),
        ),
        out_specs=(
            P("fsdp", "seq", None),
            P("fsdp", "seq", None),
            P("fsdp"),
            P("fsdp"),
            P("fsdp", None),
            P(None, "fsdp"),
            P("fsdp", None),
            P("fsdp"),
            P("fsdp"),
            P("fsdp"),
            P("fsdp", None),
            P("fsdp"),
            P("fsdp", None),
            P("fsdp"),
        ),
        check_vma=False,
    )
```

```python
import functools

import jax
import jax.numpy as jnp
from jax import lax
from jax.experimental import pallas as pl
from jax.experimental.pallas import tpu as pltpu
from jax.sharding import PartitionSpec as P

D = 1024
H = 16
HEAD = D // H
EPSILON = 1e-05
F32 = jnp.float32
BF16 = jnp.bfloat16
NT = (((1,), (1,)), ((), ()))
NN = (((1,), (0,)), ((), ()))
TN = (((0,), (0,)), ((), ()))


def dot(a, b, dims=NN):
    return lax.dot_general(a, b, dims, preferred_element_type=F32)


def key_start(first_query, block, longest):
    return max(0, (first_query - longest + 1) // block * block)


def masked_distance(seg_col, seg_row, k0, nk, q0, bq):
    key_at = lax.broadcasted_iota(jnp.int32, (nk, bq), 0) + k0
    query_at = lax.broadcasted_iota(jnp.int32, (nk, bq), 1) + q0
    ok = (key_at <= query_at) & (seg_col[k0 : k0 + nk, :] == seg_row[:, q0 : q0 + bq])
    return jnp.where(ok, (query_at - key_at).astype(F32), 1e32)


def only_head(values, head):
    lane = lax.broadcasted_iota(jnp.int32, values.shape, 1)
    return jnp.where(lane // HEAD == head, values, jnp.zeros_like(values))


def attention_kernel(slopes, proj, seg_col, seg_row, context, log_total, *, block, longest):
    length = proj.shape[0]
    width = proj.shape[1] // 3
    for q0 in range(0, length, block):
        k0 = key_start(q0, block, longest)
        nk = q0 + block - k0
        far = masked_distance(seg_col, seg_row, k0, nk, q0, block)
        queries = proj[q0 : q0 + block, :width] * BF16(HEAD**-0.5)
        keys = proj[k0 : k0 + nk, width : 2 * width]
        values = proj[k0 : k0 + nk, 2 * width :].T
        parts = []
        for head in range(width // HEAD):
            raw = dot(keys, only_head(queries, head), NT) - slopes[head] * far
            highest = jnp.max(raw, axis=0, keepdims=True)
            weights = jnp.exp(raw - highest)
            total = jnp.sum(weights, axis=0, keepdims=True)
            probs = (weights * (1.0 / total)).astype(BF16)
            log_total[head : head + 1, q0 : q0 + block] = highest + jnp.log(total)
            parts.append(dot(values[head * HEAD : (head + 1) * HEAD, :], probs))
        context[q0 : q0 + block, :] = jnp.concatenate(parts, axis=0).T.astype(BF16)


def attention_back_kernel(
    slopes, proj, grad, seg_col, seg_row, log_total, out, probs_all, scores_all, grad_keys, grad_values, *, block, longest
):
    length = proj.shape[0]
    width = proj.shape[1] // 3
    heads = width // HEAD
    grad_keys[...] = jnp.zeros_like(grad_keys)
    grad_values[...] = jnp.zeros_like(grad_values)
    for q0 in range(0, length, block):
        k0 = key_start(q0, block, longest)
        nk = q0 + block - k0
        far = masked_distance(seg_col, seg_row, k0, nk, q0, block)
        queries = proj[q0 : q0 + block, :width] * BF16(HEAD**-0.5)
        keys = proj[k0 : k0 + nk, width : 2 * width]
        values = proj[k0 : k0 + nk, 2 * width :]
        keys_t = keys.T
        tops = grad[q0 : q0 + block, :]
        parts, query_rows, top_rows = [], [], []
        for head in range(heads):
            query_head = only_head(queries, head)
            top_head = only_head(tops, head)
            query_rows.append(query_head)
            top_rows.append(top_head)
            raw = dot(keys, query_head, NT) - slopes[head] * far
            probs = jnp.exp(raw - log_total[head : head + 1, q0 : q0 + block])
            probs_all[:nk, head * block : (head + 1) * block] = probs.astype(BF16)
            grad_probs = dot(values, top_head, NT)
            row_sum = jnp.sum(probs * grad_probs, axis=0, keepdims=True)
            scores = (probs * (grad_probs - row_sum)).astype(BF16)
            scores_all[:nk, head * block : (head + 1) * block] = scores
            parts.append(dot(keys_t[head * HEAD : (head + 1) * HEAD, :], scores))
        grad_values[k0 : k0 + nk, :] += dot(probs_all[:nk, :], jnp.concatenate(top_rows, axis=0))
        grad_keys[k0 : k0 + nk, :] += dot(scores_all[:nk, :], jnp.concatenate(query_rows, axis=0))
        out[q0 : q0 + block, :width] = (jnp.concatenate(parts, axis=0).T * HEAD**-0.5).astype(BF16)
    out[:, width : 2 * width] = grad_keys[...].astype(BF16)
    out[:, 2 * width :] = grad_values[...].astype(BF16)


VMEM = pl.BlockSpec(memory_space=pltpu.VMEM)
SMEM = pl.BlockSpec(memory_space=pltpu.SMEM)


def attention(slopes, proj, seg_col, seg_row):
    length, wide = proj.shape
    width = wide // 3
    heads = width // HEAD
    return pl.pallas_call(
        functools.partial(attention_kernel, block=min(256, length), longest=length // 2),
        out_shape=(
            jax.ShapeDtypeStruct((length, width), BF16),
            jax.ShapeDtypeStruct((heads, length), F32),
        ),
        in_specs=[SMEM, VMEM, VMEM, VMEM],
        out_specs=(VMEM, VMEM),
        compiler_params=pltpu.CompilerParams(vmem_limit_bytes=40 * 2**20),
        cost_estimate=pl.CostEstimate(
            flops=3 * length * length * heads * HEAD, bytes_accessed=4 * length * wide, transcendentals=length * length * heads // 2
        ),
        name="attention",
    )(slopes, proj, seg_col, seg_row)


def attention_back(slopes, proj, grad, seg_col, seg_row, log_total):
    length, wide = proj.shape
    width = wide // 3
    heads = width // HEAD
    block = min(256, length)
    most = min(length, block + length // 2)
    return pl.pallas_call(
        functools.partial(attention_back_kernel, block=block, longest=length // 2),
        out_shape=jax.ShapeDtypeStruct((length, wide), BF16),
        in_specs=[SMEM, VMEM, VMEM, VMEM, VMEM, VMEM],
        out_specs=VMEM,
        scratch_shapes=[
            pltpu.VMEM((most, heads * block), BF16),
            pltpu.VMEM((most, heads * block), BF16),
            pltpu.VMEM((length, width), F32),
            pltpu.VMEM((length, width), F32),
        ],
        compiler_params=pltpu.CompilerParams(vmem_limit_bytes=40 * 2**20),
        cost_estimate=pl.CostEstimate(
            flops=48 * length * length * heads * HEAD, bytes_accessed=6 * length * wide, transcendentals=0
        ),
        name="attention_back",
    )(slopes, proj, grad, seg_col, seg_row, log_total)


def copy_kernel(plan, inputs, position, *refs):
    for source, target in plan(position, refs[:inputs], refs[inputs:]):
        target[...] = source[...]


def copy_call(name, plan, position, operands, shapes):
    return pl.pallas_call(
        functools.partial(copy_kernel, plan, len(operands)),
        out_shape=tuple(jax.ShapeDtypeStruct(shape, BF16) for shape in shapes),
        in_specs=[SMEM] + [VMEM] * len(operands),
        out_specs=tuple(VMEM for shape in shapes),
        compiler_params=pltpu.CompilerParams(vmem_limit_bytes=40 * 2**20),
        cost_estimate=pl.CostEstimate(flops=0, bytes_accessed=4 * sum(o.size for o in operands), transcendentals=0),
        name=name,
    )(position, *operands)


def widen_columns_kernel(pieces, out, sums, added, *, blocks, rows):
    count = pieces.shape[0]
    columns = sums.shape[1]
    width = columns // blocks
    for k in range(count):
        for j in range(blocks):
            at = (j * count + k) * width
            out[:, at : at + width] = pieces[k, :rows, j * width : (j + 1) * width].astype(F32)
    sums[...] = tree_sum([pieces[k, rows:, :columns].astype(F32) for k in range(count)])
    added[...] = tree_sum([pieces[k, :rows, columns:].astype(F32) for k in range(count)])


def widen_feed_kernel(pieces, up, down, *, up_rows, blocks):
    count = pieces.shape[0]
    part, wide = up.shape
    width = wide // (blocks * count)
    own = down.shape[0] // count
    for k in range(count):
        values = pieces[k, :up_rows, :].astype(F32).reshape(part, blocks * width)
        for j in range(blocks):
            at = (j * count + k) * width
            up[:, at : at + width] = values[:, j * width : (j + 1) * width]
        down[k * own : (k + 1) * own, :] = pieces[k, up_rows:, :].astype(F32)


def project_kernel(seen, weights, gain, shift, bias, projected, normed, xhat):
    values = seen[: normed.shape[0], :].astype(F32)
    center, unused_rate = stats(values)
    xhat[...] = center.astype(BF16)
    low = (center * gain[...] + shift[...]).astype(BF16)
    normed[...] = low
    projected[...] = (dot(low, weights[...]) + bias[...]).astype(BF16)


def project(seen, weights, gain, shift, bias, rows):
    shards, height, width = seen.shape
    wide = weights.shape[1]

    def whole(shape):
        return pl.BlockSpec(shape, lambda i: (0, 0))

    return pl.pallas_call(
        project_kernel,
        grid=(shards,),
        in_specs=[
            pl.BlockSpec((None, height, width), lambda i: (i, 0, 0)),
            whole((width, wide)),
            whole((1, width)),
            whole((1, width)),
            whole((1, wide)),
        ],
        out_specs=(
            pl.BlockSpec((rows, wide), lambda i: (i, 0)),
            pl.BlockSpec((rows, width), lambda i: (i, 0)),
            pl.BlockSpec((rows, width), lambda i: (i, 0)),
        ),
        out_shape=(
            jax.ShapeDtypeStruct((shards * rows, wide), BF16),
            jax.ShapeDtypeStruct((shards * rows, width), BF16),
            jax.ShapeDtypeStruct((shards * rows, width), BF16),
        ),
        compiler_params=pltpu.CompilerParams(vmem_limit_bytes=40 * 2**20),
        cost_estimate=pl.CostEstimate(
            flops=2 * shards * rows * width * wide, bytes_accessed=8 * shards * rows * width, transcendentals=0
        ),
        name="project",
    )(seen, weights, gain[None], shift[None], bias[None])


def feed_kernel(normed, top, up, down, bias, activated, grad_upward, back, bias_sum):
    weights = up[...].reshape(normed.shape[1], -1)
    upward = dot(normed[...], weights) + bias[...]
    grad_act = dot(top[...], down[...].reshape(-1, top.shape[1]), NT)
    square = upward * upward
    slope = 0.7978845608028654
    bend = jnp.tanh(slope * upward * (1.0 + 0.044715 * square))
    half = 0.5 * (1.0 + bend)
    activated[...] = (upward * half).astype(BF16)
    rise = half + 0.5 * slope * upward * (1.0 - bend * bend) * (1.0 + 0.134145 * square)
    low = (grad_act * rise).astype(BF16)
    grad_upward[...] = low
    back[...] = dot(low, weights, NT).astype(BF16)

    @pl.when(pl.program_id(0) == 0)
    def clear():
        bias_sum[...] = jnp.zeros_like(bias_sum)

    bias_sum[...] += jnp.sum(low.astype(F32), axis=0, keepdims=True)


def feed_forward(normed, top, up, down, up_shape, down_shape, down_place, bias):
    length, width = normed.shape
    rows = min(256, length)
    hidden = bias.shape[0]

    def part(columns):
        return pl.BlockSpec((rows, columns), lambda i: (i, 0))

    return pl.pallas_call(
        feed_kernel,
        grid=(length // rows,),
        in_specs=[
            part(width),
            part(width),
            pl.BlockSpec(up_shape, lambda i: (0, 0, 0)),
            pl.BlockSpec(down_shape, lambda i: (0, down_place, 0)),
            pl.BlockSpec((1, hidden), lambda i: (0, 0)),
        ],
        out_specs=(
            part(hidden),
            part(hidden),
            part(width),
            pl.BlockSpec((1, hidden), lambda i: (0, 0)),
        ),
        out_shape=(
            jax.ShapeDtypeStruct((length, hidden), BF16),
            jax.ShapeDtypeStruct((length, hidden), BF16),
            jax.ShapeDtypeStruct((length, width), BF16),
            jax.ShapeDtypeStruct((1, hidden), F32),
        ),
        compiler_params=pltpu.CompilerParams(vmem_limit_bytes=48 * 2**20),
        cost_estimate=pl.CostEstimate(
            flops=6 * length * width * hidden, bytes_accessed=12 * length * width, transcendentals=length * hidden
        ),
        name="feed_forward",
    )(normed, top, up, down, bias[None])


def stats(values):
    center = values - jnp.mean(values, axis=-1, keepdims=True)
    spread = jnp.mean(center * center, axis=-1, keepdims=True)
    rate = lax.rsqrt(spread + EPSILON)
    return center * rate, rate


def norm_back(grad, xhat, rate, gain):
    a = grad * gain
    return rate * (
        a - jnp.mean(a, axis=-1, keepdims=True) - xhat * jnp.mean(a * xhat, axis=-1, keepdims=True)
    )


def tree_sum(terms):
    while len(terms) > 1:
        terms = [a + b for a, b in zip(terms[::2], terms[1::2])]
    return terms[0]


def together(*values):
    return lax.optimization_barrier(values)


def body(
    seq_size,
    fsdp_size,
    hidden_in,
    segment_ids,
    ln1_gain,
    ln1_bias,
    w_qkv,
    b_qv,
    w_out,
    b_out,
    ln2_gain,
    ln2_bias,
    w_up,
    b_up,
    w_down,
    b_down,
    cotangent,
):
    S, F, Z = seq_size, fsdp_size, fsdp_size // 2
    s = lax.axis_index("seq")
    f = lax.axis_index("fsdp")
    z, core = f // 2, f % 2

    def fsdp_x(x, k):
        return lax.ppermute(x, "fsdp", [(i, i ^ k) for i in range(F)])

    def put(buf, value, *index):
        index = tuple(index) + (0,) * (buf.ndim - len(index))
        return lax.dynamic_update_slice(buf, value, index)

    def spread_z(piece):
        return [piece] + [fsdp_x(piece, 2 * k) for k in range(1, Z)]

    def spread_core(own):
        return own, fsdp_x(jnp.stack(own), 1)

    def join_fsdp(name, pair, heights):
        own, other = pair
        columns = own[0].shape[1]
        ends = [sum(heights[: i + 1]) for i in range(len(heights))]

        def plan(position, ins, outs):
            for k in range(Z):
                for source, place in ((ins[k], 2 * k), (ins[Z].at[k], 2 * k + 1)):
                    for end, height, out in zip(ends, heights, outs):
                        yield source.at[end - height : end, :], out.at[position[1] ^ place]

        return copy_call(
            name, plan, place_now, own + [other], [(F, h, columns) for h in heights]
        )

    def exchange_seq(x):
        return lax.all_to_all(x, "seq", 0, 0)

    def reduce_core(partials):
        def half(index):
            return jnp.concatenate(
                [
                    lax.dynamic_index_in_dim(p.reshape(Z, 2, *p.shape[1:]), index, 1, keepdims=False)
                    for p in partials
                ],
                axis=1,
            )

        other = fsdp_x(half(1 - core), 1)
        kept = half(core)

        def block(index):
            return lax.dynamic_index_in_dim(kept, index, 0, keepdims=False).astype(
                F32
            ) + lax.dynamic_index_in_dim(other, index, 0, keepdims=False).astype(F32)

        return [block(z ^ k).astype(BF16) for k in range(Z)]

    def reduce_z(blocks):
        return [blocks[0]] + [fsdp_x(blocks[k], 2 * k) for k in range(1, Z)]

    def total(seen):
        return tree_sum([x.astype(F32) for x in seen]).astype(BF16)

    own_rows = hidden_in.shape[1]
    length = own_rows * S
    width = D // S
    heads = width // HEAD
    part = D // F
    ff_part = b_up.shape[0]
    ff_own = ff_part // S
    hidden = hidden_in[0]
    top = cotangent[0]

    place_now = jnp.stack([s, f])
    wide = 3 * width
    tall = ff_part // part
    extra = 16
    small = jnp.concatenate(
        [
            v.reshape(-1, part)
            for v in (ln1_gain, ln1_bias, b_qv, b_out, ln2_gain, ln2_bias, b_down, b_up)
        ],
        axis=0,
    )
    small = jnp.pad(small, ((0, extra - small.shape[0]), (0, wide - part)))

    aligned = ff_own % 128 == 0
    up_rows = part * F * ff_own // D
    up_source = w_up
    if not aligned:
        up_source = lax.dynamic_index_in_dim(
            w_up.reshape(part, F, S, ff_own), s, 2, keepdims=False
        ).reshape(up_rows, D)

    def pack_qkv_plan(position, ins, outs):
        at = position[0]
        for j in range(3):
            yield (
                ins[0].at[:, pl.ds(pl.multiple_of(j * D + at * width, width), width)],
                outs[0].at[:part, j * width : (j + 1) * width],
            )
        yield ins[1], outs[0].at[part:, :]

    def pack_rest_plan(position, ins, outs):
        at = position[0]
        if aligned:
            for j in range(F):
                yield (
                    ins[0].at[:, pl.ds(pl.multiple_of(j * ff_part + at * ff_own, ff_own), ff_own)],
                    outs[0].at[:up_rows, j * ff_own : (j + 1) * ff_own],
                )
        else:
            yield ins[0], outs[0].at[:up_rows, :]
        yield (
            ins[1].at[pl.ds(pl.multiple_of(at * ff_own, ff_own), ff_own), :],
            outs[0].at[up_rows:, :],
        )

    def to_all(x):
        return jnp.broadcast_to(x[None], (S, *x.shape))

    (qkv_piece,) = copy_call(
        "pack_qkv", pack_qkv_plan, place_now, [w_qkv, small], [(part + extra, wide)]
    )
    docs_row = jnp.pad(segment_ids.astype(BF16), ((0, 15), (0, D - own_rows)))
    packed, qkv_piece = together(
        to_all(jnp.concatenate([hidden, docs_row], axis=0)), qkv_piece
    )
    hidden_seen = exchange_seq(packed)
    qkv_own = spread_z(qkv_piece)
    hidden_seen, top = together(hidden_seen, top)
    (rest_piece,) = copy_call(
        "pack_rest",
        pack_rest_plan,
        place_now,
        [up_source, w_down],
        [(up_rows + ff_own, D)],
    )
    top_sent, rest_piece, w_out, *qkv_own = together(to_all(top), rest_piece, w_out, *qkv_own)
    qkv_pair = spread_core(qkv_own)
    full_out = lax.all_gather(w_out, "fsdp", axis=0, tiled=True)
    rest = lax.all_gather(rest_piece, "fsdp", axis=0)
    top_all = exchange_seq(top_sent).reshape(length, D)
    doc_ids = hidden_seen[:, own_rows, :own_rows].astype(jnp.int32).reshape(1, length)
    doc_col = doc_ids.reshape(length, 1)

    full_qkv, small_all = join_fsdp("join_qkv", qkv_pair, [part, extra])
    full_qkv = full_qkv.reshape(D, wide)
    small_all = small_all[:, :, :part].astype(F32)
    vectors = [small_all[:, i].reshape(D) for i in range(8)]
    gain_one, shift_one, bias_q, bias_v, bias_out, gain_two, shift_two, bias_down = vectors
    bias_up = small_all[:, 8 : 8 + tall].reshape(F, S, ff_own)
    bias_up = lax.dynamic_index_in_dim(bias_up, s, 1, keepdims=False).reshape(F * ff_own)

    tokens = hidden.astype(F32)
    own_bias = jnp.concatenate(
        [
            lax.dynamic_slice_in_dim(bias_q, s * width, width),
            jnp.zeros((width,), F32),
            lax.dynamic_slice_in_dim(bias_v, s * width, width),
        ]
    )
    projected, normed_all, xhat_all = project(
        hidden_seen, full_qkv, gain_one, shift_one, own_bias, own_rows
    )
    slopes = 2.0 ** (-8.0 * (s * heads + jnp.arange(heads) + 1).astype(F32) / H)
    context, log_total = attention(slopes, projected, doc_col, doc_ids)

    context, top_all = together(context, top_all)
    context_seen = exchange_seq(context.reshape(S, own_rows, width))
    gathered = jnp.concatenate([context_seen[k] for k in range(S)], axis=1)
    full_up = rest[:, :up_rows].reshape(D, F * ff_own)
    full_down = rest[:, up_rows:].reshape(F * ff_own, D)
    first_sum = tokens + dot(gathered, full_out) + bias_out
    xhat_two, rate_two = stats(first_sum)
    normed_two = (xhat_two * gain_two + shift_two).astype(BF16)
    normed_two_all = exchange_seq(to_all(normed_two)).reshape(length, D)
    if F * ff_own == D and up_rows == ff_own:
        feed_weights = (rest, rest, (F, part, D), (F, ff_own, D), 1)
    else:
        feed_weights = (
            full_up.reshape(F, part, F * ff_own),
            full_down.reshape(F, ff_own, D),
            (F, part, F * ff_own),
            (F, ff_own, D),
            0,
        )
    activated, grad_upward, grad_normed_two, bias_up_sum = feed_forward(
        normed_two_all, top_all, *feed_weights, bias_up
    )

    def to_tokens(partial):
        return exchange_seq(partial.astype(BF16).reshape(S, own_rows, D))

    def token_sum(seen):
        return tree_sum([seen[k].astype(F32) for k in range(S)])

    def owners(partial, columns):
        return partial.astype(BF16).reshape(F, -1, columns)

    grad_upward, t_two_sent, activated = together(grad_upward, grad_normed_two, activated)
    t_two_seen = to_tokens(t_two_sent)

    def reduce_owner(partial):
        return lax.psum_scatter(partial.astype(BF16), "fsdp", scatter_dimension=0, tiled=True)

    feed_part = jnp.concatenate(
        [
            owners(dot(normed_two_all, grad_upward, TN).reshape(F * up_rows, D), D),
            owners(dot(activated, top_all, TN), D),
        ],
        axis=1,
    ).reshape(F * (up_rows + ff_own), D)
    result_part = dot(activated, full_down).astype(BF16)
    t_two_seen, feed_part, result_part = together(t_two_seen, feed_part, result_part)
    feed_mine = reduce_owner(feed_part)
    t_two = token_sum(t_two_seen)
    grad_top = top.astype(F32)
    grad_first = grad_top + norm_back(t_two, xhat_two, rate_two, gain_two)
    grad_attended = grad_first.astype(BF16)
    grad_context = dot(grad_attended, full_out, NT).astype(BF16)
    grad_heads = exchange_seq(
        jnp.stack([grad_context[:, k * width : (k + 1) * width] for k in range(S)])
    ).reshape(length, width)

    out_part = dot(gathered, grad_attended, TN).astype(BF16)
    grad_heads, result_part, out_part = together(grad_heads, result_part, out_part)
    out_mine = reduce_owner(out_part)
    result_seen = to_tokens(result_part)
    grad_projected = attention_back(slopes, projected, grad_heads, doc_col, doc_ids, log_total)
    t_part = dot(grad_projected, full_qkv, NT).astype(BF16)
    t_part, grad_projected, result_seen = together(t_part, grad_projected, result_seen)
    t_one_seen = to_tokens(t_part)
    output = (first_sum + token_sum(result_seen) + bias_down).astype(BF16)[None]

    def own_columns(values):
        return put(jnp.zeros((D,), F32), values, s * width)

    bias_sums = jnp.sum(grad_projected.astype(F32), axis=0)
    grad_bup = bias_up_sum.reshape(F, 1, ff_own)
    low_t = t_part.astype(F32)
    rows = jnp.stack(
        [
            v.reshape(F, part)
            for v in (
                jnp.sum(low_t * xhat_all.astype(F32), axis=0),
                jnp.sum(low_t, axis=0),
                own_columns(bias_sums[:width]),
                own_columns(bias_sums[2 * width :]),
                jnp.sum(grad_attended.astype(F32), axis=0),
                jnp.sum(t_two * xhat_two, axis=0),
                jnp.sum(t_two, axis=0),
                jnp.sum(grad_top, axis=0),
            )
        ],
        axis=1,
    )
    bup_rows = put(jnp.zeros((F, S, ff_own), F32), grad_bup, 0, s).reshape(F, tall, part)
    rows = jnp.concatenate([rows, bup_rows], axis=1)
    rows = jnp.pad(rows, ((0, 0), (0, extra - rows.shape[1]), (0, wide - part))).astype(BF16)
    qkv_blocks = reduce_core([owners(dot(normed_all, grad_projected, TN), wide), rows])
    qkv_sent = reduce_z(qkv_blocks)
    t_one_seen, feed_sent, *unused_blocks = together(t_one_seen, to_all(feed_mine), *qkv_blocks)
    t_one = token_sum(t_one_seen)
    xhat_one, rate_one = stats(tokens)
    grad_input = (grad_first + norm_back(t_one, xhat_one, rate_one, gain_one)).astype(BF16)[None]


    feed_seen = exchange_seq(feed_sent)
    feed_seen, out_mine, *qkv_sent = together(feed_seen, out_mine, *qkv_sent)
    sum_up, sum_down = pl.pallas_call(
        functools.partial(widen_feed_kernel, up_rows=up_rows, blocks=F),
        out_shape=(
            jax.ShapeDtypeStruct((part, F * ff_part), F32),
            jax.ShapeDtypeStruct((ff_part, D), F32),
        ),
        in_specs=[VMEM],
        out_specs=(VMEM, VMEM),
        compiler_params=pltpu.CompilerParams(vmem_limit_bytes=40 * 2**20),
        name="widen_feed",
    )(feed_seen)
    out_tall = jnp.pad(out_mine, ((0, extra), (0, 0)))
    last_seen = exchange_seq(to_all(jnp.concatenate([total(qkv_sent), out_tall], axis=1)))
    sum_qkv, mine, sum_out = pl.pallas_call(
        functools.partial(widen_columns_kernel, blocks=3, rows=part),
        out_shape=(
            jax.ShapeDtypeStruct((part, 3 * D), F32),
            jax.ShapeDtypeStruct((extra, wide), F32),
            jax.ShapeDtypeStruct((part, D), F32),
        ),
        in_specs=[VMEM],
        out_specs=(VMEM, VMEM, VMEM),
        compiler_params=pltpu.CompilerParams(vmem_limit_bytes=40 * 2**20),
        name="widen_qkv",
    )(last_seen)
    pieces = [mine[i, :part] for i in range(8)]

    return (
        output,
        grad_input,
        pieces[0],
        pieces[1],
        sum_qkv,
        jnp.stack([pieces[2], pieces[3]]),
        sum_out,
        pieces[4],
        pieces[5],
        pieces[6],
        sum_up.reshape(part, F * ff_part),
        mine[8 : 8 + tall, :part].reshape(ff_part),
        sum_down,
        pieces[7],
    )


def solution(mesh):
    return jax.shard_map(
        functools.partial(body, mesh.shape["seq"], mesh.shape["fsdp"]),
        mesh=mesh,
        in_specs=(
            P("fsdp", "seq", None),
            P("fsdp", "seq"),
            P("fsdp"),
            P("fsdp"),
            P("fsdp", None),
            P(None, "fsdp"),
            P("fsdp", None),
            P("fsdp"),
            P("fsdp"),
            P("fsdp"),
            P("fsdp", None),
            P("fsdp"),
            P("fsdp", None),
            P("fsdp"),
            P("fsdp", "seq", None),
        ),
        out_specs=(
            P("fsdp", "seq", None),
            P("fsdp", "seq", None),
            P("fsdp"),
            P("fsdp"),
            P("fsdp", None),
            P(None, "fsdp"),
            P("fsdp", None),
            P("fsdp"),
            P("fsdp"),
            P("fsdp"),
            P("fsdp", None),
            P("fsdp"),
            P("fsdp", None),
            P("fsdp"),
        ),
        check_vma=False,
    )
```

```python
import functools

import jax
import jax.numpy as jnp
from jax import lax
from jax.experimental import pallas as pl
from jax.experimental.pallas import tpu as pltpu
from jax.sharding import PartitionSpec as P

D = 1024
H = 16
HEAD = D // H
EPSILON = 1e-05
F32 = jnp.float32
BF16 = jnp.bfloat16
NT = (((1,), (1,)), ((), ()))
NN = (((1,), (0,)), ((), ()))
TN = (((0,), (0,)), ((), ()))


def dot(a, b, dims=NN):
    return lax.dot_general(a, b, dims, preferred_element_type=F32)


def key_start(first_query, block, longest):
    return max(0, (first_query - longest + 1) // block * block)


def masked_distance(seg_col, seg_row, k0, nk, q0, bq):
    key_at = lax.broadcasted_iota(jnp.int32, (nk, bq), 0) + k0
    query_at = lax.broadcasted_iota(jnp.int32, (nk, bq), 1) + q0
    ok = (key_at <= query_at) & (seg_col[k0 : k0 + nk, :] == seg_row[:, q0 : q0 + bq])
    return jnp.where(ok, (query_at - key_at).astype(F32), 1e32)


def only_head(values, head):
    lane = lax.broadcasted_iota(jnp.int32, values.shape, 1)
    return jnp.where(lane // HEAD == head, values, jnp.zeros_like(values))


def attention_kernel(slopes, proj, seg_col, seg_row, context, log_total, *, block, longest):
    length = proj.shape[0]
    width = proj.shape[1] // 3
    for q0 in range(0, length, block):
        k0 = key_start(q0, block, longest)
        nk = q0 + block - k0
        far = masked_distance(seg_col, seg_row, k0, nk, q0, block)
        queries = proj[q0 : q0 + block, :width] * BF16(HEAD**-0.5)
        keys = proj[k0 : k0 + nk, width : 2 * width]
        values = proj[k0 : k0 + nk, 2 * width :].T
        parts = []
        for head in range(width // HEAD):
            raw = dot(keys, only_head(queries, head), NT) - slopes[head] * far
            highest = jnp.max(raw, axis=0, keepdims=True)
            weights = jnp.exp(raw - highest)
            total = jnp.sum(weights, axis=0, keepdims=True)
            probs = (weights * (1.0 / total)).astype(BF16)
            log_total[head : head + 1, q0 : q0 + block] = highest + jnp.log(total)
            parts.append(dot(values[head * HEAD : (head + 1) * HEAD, :], probs))
        context[q0 : q0 + block, :] = jnp.concatenate(parts, axis=0).T.astype(BF16)


def attention_back_kernel(
    slopes, proj, grad, seg_col, seg_row, log_total, out, probs_all, scores_all, grad_keys, grad_values, *, block, longest
):
    length = proj.shape[0]
    width = proj.shape[1] // 3
    heads = width // HEAD
    grad_keys[...] = jnp.zeros_like(grad_keys)
    grad_values[...] = jnp.zeros_like(grad_values)
    for q0 in range(0, length, block):
        k0 = key_start(q0, block, longest)
        nk = q0 + block - k0
        far = masked_distance(seg_col, seg_row, k0, nk, q0, block)
        queries = proj[q0 : q0 + block, :width] * BF16(HEAD**-0.5)
        keys = proj[k0 : k0 + nk, width : 2 * width]
        values = proj[k0 : k0 + nk, 2 * width :]
        keys_t = keys.T
        tops = grad[q0 : q0 + block, :]
        parts, query_rows, top_rows = [], [], []
        for head in range(heads):
            query_head = only_head(queries, head)
            top_head = only_head(tops, head)
            query_rows.append(query_head)
            top_rows.append(top_head)
            raw = dot(keys, query_head, NT) - slopes[head] * far
            probs = jnp.exp(raw - log_total[head : head + 1, q0 : q0 + block])
            probs_all[:nk, head * block : (head + 1) * block] = probs.astype(BF16)
            grad_probs = dot(values, top_head, NT)
            row_sum = jnp.sum(probs * grad_probs, axis=0, keepdims=True)
            scores = (probs * (grad_probs - row_sum)).astype(BF16)
            scores_all[:nk, head * block : (head + 1) * block] = scores
            parts.append(dot(keys_t[head * HEAD : (head + 1) * HEAD, :], scores))
        grad_values[k0 : k0 + nk, :] += dot(probs_all[:nk, :], jnp.concatenate(top_rows, axis=0))
        grad_keys[k0 : k0 + nk, :] += dot(scores_all[:nk, :], jnp.concatenate(query_rows, axis=0))
        out[q0 : q0 + block, :width] = (jnp.concatenate(parts, axis=0).T * HEAD**-0.5).astype(BF16)
    out[:, width : 2 * width] = grad_keys[...].astype(BF16)
    out[:, 2 * width :] = grad_values[...].astype(BF16)


VMEM = pl.BlockSpec(memory_space=pltpu.VMEM)
SMEM = pl.BlockSpec(memory_space=pltpu.SMEM)


def attention(slopes, proj, seg_col, seg_row):
    length, wide = proj.shape
    width = wide // 3
    heads = width // HEAD
    return pl.pallas_call(
        functools.partial(attention_kernel, block=min(256, length), longest=length // 2),
        out_shape=(
            jax.ShapeDtypeStruct((length, width), BF16),
            jax.ShapeDtypeStruct((heads, length), F32),
        ),
        in_specs=[SMEM, VMEM, VMEM, VMEM],
        out_specs=(VMEM, VMEM),
        compiler_params=pltpu.CompilerParams(vmem_limit_bytes=40 * 2**20),
        cost_estimate=pl.CostEstimate(
            flops=3 * length * length * heads * HEAD, bytes_accessed=4 * length * wide, transcendentals=length * length * heads // 2
        ),
        name="attention",
    )(slopes, proj, seg_col, seg_row)


def attention_back(slopes, proj, grad, seg_col, seg_row, log_total):
    length, wide = proj.shape
    width = wide // 3
    heads = width // HEAD
    block = min(256, length)
    most = min(length, block + length // 2)
    return pl.pallas_call(
        functools.partial(attention_back_kernel, block=block, longest=length // 2),
        out_shape=jax.ShapeDtypeStruct((length, wide), BF16),
        in_specs=[SMEM, VMEM, VMEM, VMEM, VMEM, VMEM],
        out_specs=VMEM,
        scratch_shapes=[
            pltpu.VMEM((most, heads * block), BF16),
            pltpu.VMEM((most, heads * block), BF16),
            pltpu.VMEM((length, width), F32),
            pltpu.VMEM((length, width), F32),
        ],
        compiler_params=pltpu.CompilerParams(vmem_limit_bytes=40 * 2**20),
        cost_estimate=pl.CostEstimate(
            flops=48 * length * length * heads * HEAD, bytes_accessed=6 * length * wide, transcendentals=0
        ),
        name="attention_back",
    )(slopes, proj, grad, seg_col, seg_row, log_total)


def copy_kernel(plan, inputs, position, *refs):
    for source, target in plan(position, refs[:inputs], refs[inputs:]):
        target[...] = source[...]


def copy_call(name, plan, position, operands, shapes):
    return pl.pallas_call(
        functools.partial(copy_kernel, plan, len(operands)),
        out_shape=tuple(jax.ShapeDtypeStruct(shape, BF16) for shape in shapes),
        in_specs=[SMEM] + [VMEM] * len(operands),
        out_specs=tuple(VMEM for shape in shapes),
        compiler_params=pltpu.CompilerParams(vmem_limit_bytes=40 * 2**20),
        cost_estimate=pl.CostEstimate(flops=0, bytes_accessed=4 * sum(o.size for o in operands), transcendentals=0),
        name=name,
    )(position, *operands)


def widen_columns_kernel(pieces, out, sums, added, *, blocks, rows):
    count = pieces.shape[0]
    columns = sums.shape[1]
    width = columns // blocks
    for k in range(count):
        for j in range(blocks):
            at = (j * count + k) * width
            out[:, at : at + width] = pieces[k, :rows, j * width : (j + 1) * width].astype(F32)
    sums[...] = tree_sum([pieces[k, rows:, :columns].astype(F32) for k in range(count)])
    added[...] = tree_sum([pieces[k, :rows, columns:].astype(F32) for k in range(count)])


def widen_feed_kernel(pieces, up, down, *, up_rows, blocks):
    count = pieces.shape[0]
    part, wide = up.shape
    width = wide // (blocks * count)
    own = down.shape[0] // count
    for k in range(count):
        values = pieces[k, :up_rows, :].astype(F32).reshape(part, blocks * width)
        for j in range(blocks):
            at = (j * count + k) * width
            up[:, at : at + width] = values[:, j * width : (j + 1) * width]
        down[k * own : (k + 1) * own, :] = pieces[k, up_rows:, :].astype(F32)


def project_kernel(seen, weights, gain, shift, bias, projected, normed, xhat):
    values = seen[: normed.shape[0], :].astype(F32)
    center, unused_rate = stats(values)
    xhat[...] = center.astype(BF16)
    low = (center * gain[...] + shift[...]).astype(BF16)
    normed[...] = low
    projected[...] = (dot(low, weights[...]) + bias[...]).astype(BF16)


def project(seen, weights, gain, shift, bias, rows):
    shards, height, width = seen.shape
    wide = weights.shape[1]

    def whole(shape):
        return pl.BlockSpec(shape, lambda i: (0, 0))

    return pl.pallas_call(
        project_kernel,
        grid=(shards,),
        in_specs=[
            pl.BlockSpec((None, height, width), lambda i: (i, 0, 0)),
            whole((width, wide)),
            whole((1, width)),
            whole((1, width)),
            whole((1, wide)),
        ],
        out_specs=(
            pl.BlockSpec((rows, wide), lambda i: (i, 0)),
            pl.BlockSpec((rows, width), lambda i: (i, 0)),
            pl.BlockSpec((rows, width), lambda i: (i, 0)),
        ),
        out_shape=(
            jax.ShapeDtypeStruct((shards * rows, wide), BF16),
            jax.ShapeDtypeStruct((shards * rows, width), BF16),
            jax.ShapeDtypeStruct((shards * rows, width), BF16),
        ),
        compiler_params=pltpu.CompilerParams(vmem_limit_bytes=40 * 2**20),
        cost_estimate=pl.CostEstimate(
            flops=2 * shards * rows * width * wide, bytes_accessed=8 * shards * rows * width, transcendentals=0
        ),
        name="project",
    )(seen, weights, gain[None], shift[None], bias[None])


def feed_kernel(normed, top, up, down, bias, activated, grad_upward, back, bias_sum):
    weights = up[...].reshape(normed.shape[1], -1)
    upward = dot(normed[...], weights) + bias[...]
    grad_act = dot(top[...], down[...].reshape(-1, top.shape[1]), NT)
    square = upward * upward
    slope = 0.7978845608028654
    bend = jnp.tanh(slope * upward * (1.0 + 0.044715 * square))
    half = 0.5 * (1.0 + bend)
    activated[...] = (upward * half).astype(BF16)
    rise = half + 0.5 * slope * upward * (1.0 - bend * bend) * (1.0 + 0.134145 * square)
    low = (grad_act * rise).astype(BF16)
    grad_upward[...] = low
    back[...] = dot(low, weights, NT).astype(BF16)

    @pl.when(pl.program_id(0) == 0)
    def clear():
        bias_sum[...] = jnp.zeros_like(bias_sum)

    bias_sum[...] += jnp.sum(low.astype(F32), axis=0, keepdims=True)


def feed_forward(normed, top, up, down, up_shape, down_shape, down_place, bias):
    length, width = normed.shape
    rows = min(256, length)
    hidden = bias.shape[0]

    def part(columns):
        return pl.BlockSpec((rows, columns), lambda i: (i, 0))

    return pl.pallas_call(
        feed_kernel,
        grid=(length // rows,),
        in_specs=[
            part(width),
            part(width),
            pl.BlockSpec(up_shape, lambda i: (0, 0, 0)),
            pl.BlockSpec(down_shape, lambda i: (0, down_place, 0)),
            pl.BlockSpec((1, hidden), lambda i: (0, 0)),
        ],
        out_specs=(
            part(hidden),
            part(hidden),
            part(width),
            pl.BlockSpec((1, hidden), lambda i: (0, 0)),
        ),
        out_shape=(
            jax.ShapeDtypeStruct((length, hidden), BF16),
            jax.ShapeDtypeStruct((length, hidden), BF16),
            jax.ShapeDtypeStruct((length, width), BF16),
            jax.ShapeDtypeStruct((1, hidden), F32),
        ),
        compiler_params=pltpu.CompilerParams(vmem_limit_bytes=48 * 2**20),
        cost_estimate=pl.CostEstimate(
            flops=6 * length * width * hidden, bytes_accessed=12 * length * width, transcendentals=length * hidden
        ),
        name="feed_forward",
    )(normed, top, up, down, bias[None])


def stats(values):
    center = values - jnp.mean(values, axis=-1, keepdims=True)
    spread = jnp.mean(center * center, axis=-1, keepdims=True)
    rate = lax.rsqrt(spread + EPSILON)
    return center * rate, rate


def norm_back(grad, xhat, rate, gain):
    a = grad * gain
    return rate * (
        a - jnp.mean(a, axis=-1, keepdims=True) - xhat * jnp.mean(a * xhat, axis=-1, keepdims=True)
    )


def tree_sum(terms):
    while len(terms) > 1:
        terms = [a + b for a, b in zip(terms[::2], terms[1::2])]
    return terms[0]


def together(*values):
    return lax.optimization_barrier(values)


def body(
    seq_size,
    fsdp_size,
    hidden_in,
    segment_ids,
    ln1_gain,
    ln1_bias,
    w_qkv,
    b_qv,
    w_out,
    b_out,
    ln2_gain,
    ln2_bias,
    w_up,
    b_up,
    w_down,
    b_down,
    cotangent,
):
    S, F, Z = seq_size, fsdp_size, fsdp_size // 2
    s = lax.axis_index("seq")
    f = lax.axis_index("fsdp")
    z, core = f // 2, f % 2

    def fsdp_x(x, k):
        return lax.ppermute(x, "fsdp", [(i, i ^ k) for i in range(F)])

    def put(buf, value, *index):
        index = tuple(index) + (0,) * (buf.ndim - len(index))
        return lax.dynamic_update_slice(buf, value, index)

    def spread_z(piece):
        return [piece] + [fsdp_x(piece, 2 * k) for k in range(1, Z)]

    def spread_core(own):
        return own, fsdp_x(jnp.stack(own), 1)

    def join_fsdp(name, pair, heights):
        own, other = pair
        columns = own[0].shape[1]
        ends = [sum(heights[: i + 1]) for i in range(len(heights))]

        def plan(position, ins, outs):
            for k in range(Z):
                for source, place in ((ins[k], 2 * k), (ins[Z].at[k], 2 * k + 1)):
                    for end, height, out in zip(ends, heights, outs):
                        yield source.at[end - height : end, :], out.at[position[1] ^ place]

        return copy_call(
            name, plan, place_now, own + [other], [(F, h, columns) for h in heights]
        )

    def exchange_seq(x):
        return lax.all_to_all(x, "seq", 0, 0)

    def reduce_core(partials):
        def half(index):
            return jnp.concatenate(
                [
                    lax.dynamic_index_in_dim(p.reshape(Z, 2, *p.shape[1:]), index, 1, keepdims=False)
                    for p in partials
                ],
                axis=1,
            )

        other = fsdp_x(half(1 - core), 1)
        kept = half(core)

        def block(index):
            return lax.dynamic_index_in_dim(kept, index, 0, keepdims=False).astype(
                F32
            ) + lax.dynamic_index_in_dim(other, index, 0, keepdims=False).astype(F32)

        return [block(z ^ k).astype(BF16) for k in range(Z)]

    def reduce_z(blocks):
        return [blocks[0]] + [fsdp_x(blocks[k], 2 * k) for k in range(1, Z)]

    def total(seen):
        return tree_sum([x.astype(F32) for x in seen]).astype(BF16)

    own_rows = hidden_in.shape[1]
    length = own_rows * S
    width = D // S
    heads = width // HEAD
    part = D // F
    ff_part = b_up.shape[0]
    ff_own = ff_part // S
    hidden = hidden_in[0]
    top = cotangent[0]

    place_now = jnp.stack([s, f])
    wide = 3 * width
    tall = ff_part // part
    extra = 16
    small = jnp.concatenate(
        [
            v.reshape(-1, part)
            for v in (ln1_gain, ln1_bias, b_qv, b_out, ln2_gain, ln2_bias, b_down, b_up)
        ],
        axis=0,
    )
    small = jnp.pad(small, ((0, extra - small.shape[0]), (0, wide - part)))

    aligned = ff_own % 128 == 0
    up_rows = part * F * ff_own // D
    up_source = w_up
    if not aligned:
        up_source = lax.dynamic_index_in_dim(
            w_up.reshape(part, F, S, ff_own), s, 2, keepdims=False
        ).reshape(up_rows, D)

    def pack_qkv_plan(position, ins, outs):
        at = position[0]
        for j in range(3):
            yield (
                ins[0].at[:, pl.ds(pl.multiple_of(j * D + at * width, width), width)],
                outs[0].at[:part, j * width : (j + 1) * width],
            )
        yield ins[1], outs[0].at[part:, :]

    def pack_rest_plan(position, ins, outs):
        at = position[0]
        if aligned:
            for j in range(F):
                yield (
                    ins[0].at[:, pl.ds(pl.multiple_of(j * ff_part + at * ff_own, ff_own), ff_own)],
                    outs[0].at[:up_rows, j * ff_own : (j + 1) * ff_own],
                )
        else:
            yield ins[0], outs[0].at[:up_rows, :]
        yield (
            ins[1].at[pl.ds(pl.multiple_of(at * ff_own, ff_own), ff_own), :],
            outs[0].at[up_rows:, :],
        )

    def to_all(x):
        return jnp.broadcast_to(x[None], (S, *x.shape))

    (qkv_piece,) = copy_call(
        "pack_qkv", pack_qkv_plan, place_now, [w_qkv, small], [(part + extra, wide)]
    )
    docs_row = jnp.pad(segment_ids.astype(BF16), ((0, 15), (0, D - own_rows)))
    packed, qkv_piece = together(
        to_all(jnp.concatenate([hidden, docs_row], axis=0)), qkv_piece
    )
    hidden_seen = exchange_seq(packed)
    qkv_own = spread_z(qkv_piece)
    hidden_seen, top = together(hidden_seen, top)
    (rest_piece,) = copy_call(
        "pack_rest",
        pack_rest_plan,
        place_now,
        [up_source, w_down],
        [(up_rows + ff_own, D)],
    )
    top_sent, rest_piece, w_out, *qkv_own = together(to_all(top), rest_piece, w_out, *qkv_own)
    qkv_pair = spread_core(qkv_own)
    full_out = lax.all_gather(w_out, "fsdp", axis=0, tiled=True)
    rest = lax.all_gather(rest_piece, "fsdp", axis=0)
    top_all = exchange_seq(top_sent).reshape(length, D)
    doc_ids = hidden_seen[:, own_rows, :own_rows].astype(jnp.int32).reshape(1, length)
    doc_col = doc_ids.reshape(length, 1)

    full_qkv, small_all = join_fsdp("join_qkv", qkv_pair, [part, extra])
    full_qkv = full_qkv.reshape(D, wide)
    small_all = small_all[:, :, :part].astype(F32)
    vectors = [small_all[:, i].reshape(D) for i in range(8)]
    gain_one, shift_one, bias_q, bias_v, bias_out, gain_two, shift_two, bias_down = vectors
    bias_up = small_all[:, 8 : 8 + tall].reshape(F, S, ff_own)
    bias_up = lax.dynamic_index_in_dim(bias_up, s, 1, keepdims=False).reshape(F * ff_own)

    tokens = hidden.astype(F32)
    own_bias = jnp.concatenate(
        [
            lax.dynamic_slice_in_dim(bias_q, s * width, width),
            jnp.zeros((width,), F32),
            lax.dynamic_slice_in_dim(bias_v, s * width, width),
        ]
    )
    projected, normed_all, xhat_all = project(
        hidden_seen, full_qkv, gain_one, shift_one, own_bias, own_rows
    )
    slopes = 2.0 ** (-8.0 * (s * heads + jnp.arange(heads) + 1).astype(F32) / H)
    context, log_total = attention(slopes, projected, doc_col, doc_ids)

    context, top_all = together(context, top_all)
    context_seen = exchange_seq(context.reshape(S, own_rows, width))
    gathered = jnp.concatenate([context_seen[k] for k in range(S)], axis=1)
    full_up = rest[:, :up_rows].reshape(D, F * ff_own)
    full_down = rest[:, up_rows:].reshape(F * ff_own, D)
    first_sum = tokens + dot(gathered, full_out) + bias_out
    xhat_two, rate_two = stats(first_sum)
    normed_two = (xhat_two * gain_two + shift_two).astype(BF16)
    normed_two_all = exchange_seq(to_all(normed_two)).reshape(length, D)
    if F * ff_own == D and up_rows == ff_own:
        feed_weights = (rest, rest, (F, part, D), (F, ff_own, D), 1)
    else:
        feed_weights = (
            full_up.reshape(F, part, F * ff_own),
            full_down.reshape(F, ff_own, D),
            (F, part, F * ff_own),
            (F, ff_own, D),
            0,
        )
    activated, grad_upward, grad_normed_two, bias_up_sum = feed_forward(
        normed_two_all, top_all, *feed_weights, bias_up
    )

    def to_tokens(partial):
        return exchange_seq(partial.astype(BF16).reshape(S, own_rows, D))

    def token_sum(seen):
        return tree_sum([seen[k].astype(F32) for k in range(S)])

    def owners(partial, columns):
        return partial.astype(BF16).reshape(F, -1, columns)

    grad_upward, t_two_sent, activated = together(grad_upward, grad_normed_two, activated)
    t_two_seen = to_tokens(t_two_sent)

    def reduce_owner(partial):
        return lax.psum_scatter(partial.astype(BF16), "fsdp", scatter_dimension=0, tiled=True)

    feed_part = jnp.concatenate(
        [
            owners(dot(normed_two_all, grad_upward, TN).reshape(F * up_rows, D), D),
            owners(dot(activated, top_all, TN), D),
        ],
        axis=1,
    ).reshape(F * (up_rows + ff_own), D)
    result_part = dot(activated, full_down).astype(BF16)
    t_two_seen, feed_part, result_part = together(t_two_seen, feed_part, result_part)
    feed_mine = reduce_owner(feed_part)
    t_two = token_sum(t_two_seen)
    grad_top = top.astype(F32)
    grad_first = grad_top + norm_back(t_two, xhat_two, rate_two, gain_two)
    grad_attended = grad_first.astype(BF16)
    grad_context = dot(grad_attended, full_out, NT).astype(BF16)
    grad_heads = exchange_seq(
        jnp.stack([grad_context[:, k * width : (k + 1) * width] for k in range(S)])
    ).reshape(length, width)

    out_part = dot(gathered, grad_attended, TN).astype(BF16)
    grad_heads, result_part, out_part = together(grad_heads, result_part, out_part)
    out_mine = reduce_owner(out_part)
    result_seen = to_tokens(result_part)
    grad_projected = attention_back(slopes, projected, grad_heads, doc_col, doc_ids, log_total)
    t_part = dot(grad_projected, full_qkv, NT).astype(BF16)
    grad_projected, result_seen = together(grad_projected, result_seen)
    t_one_seen = to_tokens(t_part)
    output = (first_sum + token_sum(result_seen) + bias_down).astype(BF16)[None]

    def own_columns(values):
        return put(jnp.zeros((D,), F32), values, s * width)

    bias_sums = jnp.sum(grad_projected.astype(F32), axis=0)
    grad_bup = bias_up_sum.reshape(F, 1, ff_own)
    low_t = t_part.astype(F32)
    rows = jnp.stack(
        [
            v.reshape(F, part)
            for v in (
                jnp.sum(low_t * xhat_all.astype(F32), axis=0),
                jnp.sum(low_t, axis=0),
                own_columns(bias_sums[:width]),
                own_columns(bias_sums[2 * width :]),
                jnp.sum(grad_attended.astype(F32), axis=0),
                jnp.sum(t_two * xhat_two, axis=0),
                jnp.sum(t_two, axis=0),
                jnp.sum(grad_top, axis=0),
            )
        ],
        axis=1,
    )
    bup_rows = put(jnp.zeros((F, S, ff_own), F32), grad_bup, 0, s).reshape(F, tall, part)
    rows = jnp.concatenate([rows, bup_rows], axis=1)
    rows = jnp.pad(rows, ((0, 0), (0, extra - rows.shape[1]), (0, wide - part))).astype(BF16)
    qkv_blocks = reduce_core([owners(dot(normed_all, grad_projected, TN), wide), rows])
    qkv_sent = reduce_z(qkv_blocks)
    t_one_seen, feed_sent, *unused_blocks = together(t_one_seen, to_all(feed_mine), *qkv_blocks)
    t_one = token_sum(t_one_seen)
    xhat_one, rate_one = stats(tokens)
    grad_input = (grad_first + norm_back(t_one, xhat_one, rate_one, gain_one)).astype(BF16)[None]


    feed_seen = exchange_seq(feed_sent)
    feed_seen, out_mine, *qkv_sent = together(feed_seen, out_mine, *qkv_sent)
    sum_up, sum_down = pl.pallas_call(
        functools.partial(widen_feed_kernel, up_rows=up_rows, blocks=F),
        out_shape=(
            jax.ShapeDtypeStruct((part, F * ff_part), F32),
            jax.ShapeDtypeStruct((ff_part, D), F32),
        ),
        in_specs=[VMEM],
        out_specs=(VMEM, VMEM),
        compiler_params=pltpu.CompilerParams(vmem_limit_bytes=40 * 2**20),
        name="widen_feed",
    )(feed_seen)
    out_tall = jnp.pad(out_mine, ((0, extra), (0, 0)))
    last_seen = exchange_seq(to_all(jnp.concatenate([total(qkv_sent), out_tall], axis=1)))
    sum_qkv, mine, sum_out = pl.pallas_call(
        functools.partial(widen_columns_kernel, blocks=3, rows=part),
        out_shape=(
            jax.ShapeDtypeStruct((part, 3 * D), F32),
            jax.ShapeDtypeStruct((extra, wide), F32),
            jax.ShapeDtypeStruct((part, D), F32),
        ),
        in_specs=[VMEM],
        out_specs=(VMEM, VMEM, VMEM),
        compiler_params=pltpu.CompilerParams(vmem_limit_bytes=40 * 2**20),
        name="widen_qkv",
    )(last_seen)
    pieces = [mine[i, :part] for i in range(8)]

    return (
        output,
        grad_input,
        pieces[0],
        pieces[1],
        sum_qkv,
        jnp.stack([pieces[2], pieces[3]]),
        sum_out,
        pieces[4],
        pieces[5],
        pieces[6],
        sum_up.reshape(part, F * ff_part),
        mine[8 : 8 + tall, :part].reshape(ff_part),
        sum_down,
        pieces[7],
    )


def solution(mesh):
    return jax.shard_map(
        functools.partial(body, mesh.shape["seq"], mesh.shape["fsdp"]),
        mesh=mesh,
        in_specs=(
            P("fsdp", "seq", None),
            P("fsdp", "seq"),
            P("fsdp"),
            P("fsdp"),
            P("fsdp", None),
            P(None, "fsdp"),
            P("fsdp", None),
            P("fsdp"),
            P("fsdp"),
            P("fsdp"),
            P("fsdp", None),
            P("fsdp"),
            P("fsdp", None),
            P("fsdp"),
            P("fsdp", "seq", None),
        ),
        out_specs=(
            P("fsdp", "seq", None),
            P("fsdp", "seq", None),
            P("fsdp"),
            P("fsdp"),
            P("fsdp", None),
            P(None, "fsdp"),
            P("fsdp", None),
            P("fsdp"),
            P("fsdp"),
            P("fsdp"),
            P("fsdp", None),
            P("fsdp"),
            P("fsdp", None),
            P("fsdp"),
        ),
        check_vma=False,
    )
```
